256 devices in a mesh: wide: 32 (over z, y), narrow: 8 (over x, core).
Axes of the slice: x: 4, y: 4, z: 8, core: 2. Of those that a mesh axis runs over, the one named last changes fastest.
Arguments:
- spins: int32 [4096, 4096], P('wide'), may hold values from -1 to 1, as said below
- weights: bfloat16 [4096, 8192], P('wide', 'narrow'), may hold values from -0.09375 to 0.09375
- field_bias: float32 [8192], P('narrow'), may hold values from -3 to 3
- energies: bfloat16 [4096], P('wide')
- panel_index: int32 [1], replicated, may hold values from 0 to 3
- diag_inverse: bfloat16 [1024, 1024], replicated, as said below
Outputs:
- grad_w: float32 [4096, 8192], P('wide', 'narrow')
- panel_factor: bfloat16 [4096, 1024], P(('wide', 'narrow'))
- update: float32 [4096], P(('wide', 'narrow'))
The draws below stay inside these ranges and needn't reach their ends.
Inputs may be any that keep to these rules, and one draw needn't show every extreme that they name: `spins`: each entry is +1 or -1. `diag_inverse`: lower triangular.
All inputs are finite; a program needn't handle non-finite values.
Results may differ from the reference program's by a relative error of at most 0.025.
Values may be sent and summed in bfloat16 or wider, within the bound.
A program may use at most 64 MiB of HBM per device.

```python
import math
import jax
import jax.numpy as jnp
from jax import lax

SPIN_SITES = 4096
HIDDEN_UNITS = 8192
PANEL_ROWS = 1024
SAMPLES_DEV = 128
SAMPLES = 4096
N_WIDE = 32


def draw_spins(key, part):
    row_index = lax.broadcasted_iota(jnp.int32, (SAMPLES, SPIN_SITES), 0)
    level = 500 + 150 * row_index // SAMPLES
    coins = jax.random.randint(key, (SAMPLES, SPIN_SITES), 0, 1000)
    return jnp.where(coins < level, 1, -1).astype(jnp.int32)


def draw_energies(key, part):
    position = jnp.arange(SAMPLES, dtype=jnp.float32) / SAMPLES
    noise = jax.random.normal(key, (SAMPLES,), jnp.float32)
    offset = 1.0 + 2.0 * position
    return (offset + noise).astype(jnp.bfloat16)


def draw_diag_inverse(key, part):
    first_key = jax.random.fold_in(key, 11)
    second_key = jax.random.fold_in(key, 23)
    row_index = lax.broadcasted_iota(jnp.int32, (PANEL_ROWS, PANEL_ROWS), 0)
    col_index = lax.broadcasted_iota(jnp.int32, (PANEL_ROWS, PANEL_ROWS), 1)
    lower = jax.random.normal(first_key, (PANEL_ROWS, PANEL_ROWS), jnp.float32) * (0.6 / math.sqrt(PANEL_ROWS))
    diagonal = jax.random.uniform(second_key, (PANEL_ROWS, PANEL_ROWS), jnp.float32, 0.6, 1.4)
    result = jnp.where(row_index > col_index, lower, jnp.where(row_index == col_index, diagonal, 0.0))
    return result.astype(jnp.bfloat16)


def steps_of(stream_key, shape, cuts, low, top_value):
    def one(dim, blocks):
        draws = jax.random.uniform(jax.random.fold_in(jax.random.fold_in(stream_key, 6), dim), (blocks,), jnp.float32, low / len(cuts), top_value / len(cuts))
        return jnp.repeat(jnp.exp(draws), shape[dim] // blocks).reshape((-1,) + (1,) * (len(shape) - dim - 1))

    gain = one(*cuts[0])
    for cut in cuts[1:]:
        gain = gain * one(*cut)
    return gain


def normal_values(stream_key, shape, deviation, reach, shards=(), kind=jnp.bfloat16):
    entries = jax.random.normal(stream_key, shape, jnp.float32) * deviation
    if len(shards) > 0:
        entries = steps_of(stream_key, shape, shards, -0.22, 0.18) * entries
    return jnp.clip(entries, min=-reach, max=reach).astype(kind)


def setup_inputs(seed: int = 0) -> dict:
    seeds = jax.random.split(jax.random.key(seed), 7)
    spins = draw_spins(jax.random.fold_in(seeds[6], 71), 0)
    weights = normal_values(seeds[1], (SPIN_SITES, HIDDEN_UNITS), SPIN_SITES ** -0.5, 0.09375, ((0, 32), (1, 8)))
    field_bias = normal_values(seeds[2], (HIDDEN_UNITS,), 0.5, 3.0, ((0, 8),), jnp.float32)
    energies = draw_energies(jax.random.fold_in(seeds[6], 71), 0)
    panel_index = jax.random.randint(seeds[4], (1,), 0, SAMPLES // PANEL_ROWS).astype(jnp.int32)
    diag_inverse = draw_diag_inverse(jax.random.fold_in(seeds[6], 71), 0)
    return dict(spins=spins, weights=weights, field_bias=field_bias, energies=energies, panel_index=panel_index, diag_inverse=diag_inverse)


def reference(spins, weights, field_bias, energies, panel_index, diag_inverse):
    spin_values = spins.astype(jnp.bfloat16)
    field_sum = jnp.dot(spin_values, weights, preferred_element_type=jnp.float32)
    fields = jnp.tanh(field_sum + field_bias[None, :]).astype(jnp.bfloat16)
    energy_mean = jnp.sum(energies.astype(jnp.float32)) / SAMPLES
    panel_block = panel_index[0].astype(jnp.int32)
    first_row = (panel_block * PANEL_ROWS).astype(jnp.int32)
    panel_spins = lax.dynamic_slice_in_dim(spin_values, first_row, PANEL_ROWS, 0)
    panel_fields = lax.dynamic_slice_in_dim(fields, first_row, PANEL_ROWS, 0)
    panel_energy = lax.dynamic_slice_in_dim(energies, first_row, PANEL_ROWS, 0)
    contract = (((1,), (1,)), ((), ()))
    spin_gram = lax.dot_general(spin_values, panel_spins, contract, preferred_element_type=jnp.float32)
    field_gram = lax.dot_general(fields, panel_fields, contract, preferred_element_type=jnp.float32)
    gram_column = (spin_gram / SPIN_SITES * (field_gram / HIDDEN_UNITS)).astype(jnp.bfloat16)
    factor_exact = lax.dot_general(gram_column, diag_inverse, contract, preferred_element_type=jnp.float32)
    energy_panel = panel_energy.astype(jnp.float32) - energy_mean
    solved_panel = jnp.dot(diag_inverse.astype(jnp.float32), energy_panel, precision=lax.Precision.HIGHEST)
    global_rows = lax.iota(jnp.int32, SAMPLES)
    relative = global_rows - first_row
    in_panel = (relative >= 0) & (relative < PANEL_ROWS)
    picked = solved_panel[jnp.clip(relative, 0, PANEL_ROWS - 1)]
    carried = jnp.dot(factor_exact, solved_panel, precision=lax.Precision.HIGHEST)
    update = jnp.where(in_panel, picked, energies.astype(jnp.float32) - energy_mean - carried)
    weighted = (fields.astype(jnp.float32) * update[:, None]).astype(jnp.bfloat16)
    block_spins = spin_values.reshape(N_WIDE, SAMPLES_DEV, SPIN_SITES)
    block_weighted = weighted.reshape(N_WIDE, SAMPLES_DEV, HIDDEN_UNITS)

    def add_block(running, pair):
        partial_term = lax.dot_general(pair[0], pair[1], (((0,), (0,)), ((), ())), preferred_element_type=jnp.float32)
        rounded = lax.optimization_barrier(partial_term.astype(jnp.bfloat16))
        return (running + rounded.astype(jnp.float32), None)
    running, _ = lax.scan(add_block, jnp.zeros((SPIN_SITES, HIDDEN_UNITS), jnp.float32), (block_spins, block_weighted))
    grad_w = running / math.sqrt(SAMPLES)
    return (grad_w, factor_exact.astype(jnp.bfloat16), update)
```

```python
import functools
import math

import jax
import jax.numpy as jnp
from jax import lax
from jax.experimental import pallas as pl
from jax.experimental.pallas import tpu as pltpu
from jax.sharding import PartitionSpec as P

SPIN_SITES = 4096
HIDDEN_UNITS = 8192
PANEL_ROWS = 1024
SAMPLES = 4096
Z, Y, X, C = 8, 4, 4, 2
Q = X * C
NEAR = (0, 1, 7, 2, 6, 3, 5, 4)
FAR = (4, 3, 5, 2, 6, 1, 7, 0)
SAME = (2, 6, 4)
MESH = pl.DeviceIdType.MESH
BF = jnp.bfloat16
F32 = jnp.float32
CONTRACT = (((1,), (1,)), ((), ()))


class Sems:
    def __init__(self):
        self.n = 0

    def take(self, n):
        self.n += n
        return self.n - n


def layout():
    s = Sems()
    names = dict(
        wz=8, wy=24, sz=3, sx=9, sc=12, ez=8, ey=4, ps=7, pf=7,
        gc=2, gx=8, gz=8, uq=8, uz=4, r1=8, r2=16, r3=8,
    )
    return {k: s.take(n) for k, n in names.items()}, s.n


SEM, NSEM = layout()


def kernel(
    spins, weights, bias, energy, panel, diag,
    grad_out, factor_out, update_out,
    s32, sp, wg, dg, f5, ft, eg, psp, pf,
    gsend, gkeep, grecv, xsend, xrecv, tsum, zsend, zrecv,
    u1, u2, wt, pb, r1, qb, r2, zb, r3,
    ssem, rsem, lsem,
):
    wide = lax.axis_index("wide")
    q = lax.axis_index("narrow")
    z, y = wide // Y, wide % Y
    x, c = q // C, q % C
    par, j = z % 2, z // 2
    sib = x * C + (1 - c)
    sends = []

    def at_z(zz):
        return (zz * Y + y, q)

    def at_y(k):
        return (z * Y + (y + k) % Y, q)

    def at_x(k):
        return (wide, ((x + k) % X) * C + c)

    def send(src, dst, index, device):
        copy = pltpu.make_async_remote_copy(
            src_ref=src, dst_ref=dst, send_sem=ssem.at[index], recv_sem=rsem.at[index],
            device_id=device, device_id_type=MESH,
        )
        copy.start()
        sends.append(copy)

    def arrived(dst, index):
        pltpu.make_async_remote_copy(
            src_ref=dst, dst_ref=dst, send_sem=ssem.at[index], recv_sem=rsem.at[index],
            device_id=(wide, sib), device_id_type=MESH,
        ).wait_recv()

    def load_spins(k):
        return pltpu.make_async_copy(spins.at[:, pl.ds(pl.multiple_of(k * 512, 512), 512)], s32.at[k], lsem.at[k])

    for d in range(Q):
        load_spins((q + d) % Q).start()
    my_w = weights.at[:, pl.ds(pl.multiple_of(j * 256, 256), 256)]
    load_w = pltpu.make_async_copy(my_w, wg.at[wide], lsem.at[8])
    load_w.start()
    load_d = pltpu.make_async_copy(diag, dg, lsem.at[9])
    load_d.start()

    barrier = pltpu.get_barrier_semaphore()
    for d in range(1, Z):
        pl.semaphore_signal(barrier, inc=1, device_id=at_z((z + d) % Z), device_id_type=MESH)
    for k in range(1, Y):
        pl.semaphore_signal(barrier, inc=1, device_id=at_y(k), device_id_type=MESH)
    for d in range(1, Q):
        pl.semaphore_signal(barrier, inc=1, device_id=(wide, (q + d) % Q), device_id_type=MESH)

    def convert(k):
        load_spins(k).wait()
        sp[k, j] = s32[k].astype(F32).astype(BF)

    convert(q)
    eg[y, z] = energy[...]
    load_w.wait()
    pl.semaphore_wait(barrier, Z + Y + Q - 3)

    def w_y(i, z1):
        chunk = wg.at[z1 * Y + y]
        send(chunk, chunk, SEM["wy"] + i, at_y(1))
        send(chunk, chunk, SEM["wy"] + 8 + i, at_y(-1 + Y))

    def w_z(off):
        zd = (z + off) % Z
        src = weights.at[:, pl.ds(pl.multiple_of((zd // 2) * 256, 256), 256)]
        send(src, wg.at[wide], SEM["wz"] + off, at_z(zd))

    def s_z(t):
        send(sp.at[q, j], sp.at[q, j], SEM["sz"] + t, at_z((z + SAME[t]) % Z))

    w_y(0, z)
    w_z(1)
    w_z(7)
    s_z(0)
    s_z(1)
    w_z(2)
    w_z(6)
    s_z(2)
    w_z(3)
    w_z(5)
    w_z(4)
    for d in range(1, Z):
        send(eg.at[y, z], eg.at[y, z], SEM["ez"] + d, at_z((z + d) % Z))
    for d in range(1, Q):
        convert((q + d) % Q)

    def w_take(i):
        z1 = (z + NEAR[i]) % Z
        arrived(wg.at[z1 * Y + y], SEM["wz"] + (Z - NEAR[i]) % Z)
        w_y(i, z1)

    def w_relay(i):
        z1 = (z + NEAR[i]) % Z
        if i % 2 == 0:
            chunk = wg.at[z1 * Y + (y + 3) % Y]
            arrived(chunk, SEM["wy"] + i)
            send(chunk, chunk, SEM["wy"] + 16 + i, at_y(1))
        else:
            chunk = wg.at[z1 * Y + (y + 1) % Y]
            arrived(chunk, SEM["wy"] + 8 + i)
            send(chunk, chunk, SEM["wy"] + 16 + i, at_y(3))

    def zi_of(t):
        return ((z + SAME[t]) % Z) // 2

    sx, sc = SEM["sx"], SEM["sc"]

    def s_take(t):
        piece = sp.at[q, zi_of(t)]
        arrived(piece, SEM["sz"] + (1, 0, 2)[t])
        send(piece, piece, sx + t, at_x(1))
        send(piece, piece, sx + 3 + t, at_x(3))
        if t == 2:
            send(piece, piece, sx + 6 + t, at_x(2))
        send(piece, piece, sc + t, (wide, sib))

    def s_cross(t, k):
        source = ((x + (3, 1, 2)[k]) % X) * C + c
        piece = sp.at[source, zi_of(t)]
        arrived(piece, sx + 3 * k + t)
        if t == 0 and k == 0:
            send(piece, piece, sx + 6 + t, at_x(1))
        if t == 1 and k == 1:
            send(piece, piece, sx + 6 + t, at_x(3))
        send(piece, piece, sc + 3 * (k + 1) + t, (wide, sib))

    p = panel[0]
    slot = par * 4 + y
    other = (1 - par) * 4 + y
    partner = z + 1 - 2 * par

    def panel_send(buf, base):
        send(buf.at[slot], buf.at[slot], base, at_z(partner))
        for k in (1, 3, 2):
            send(buf.at[slot], buf.at[slot], base + k, at_y(k))

    def panel_pass(buf, base):
        arrived(buf.at[other], base)
        for k in (1, 3, 2):
            send(buf.at[other], buf.at[other], base + 3 + k, at_y(k))

    def panel_wait(buf, base):
        for k in (1, 3, 2):
            arrived(buf.at[par * 4 + (y + 4 - k) % 4], base + k)
            arrived(buf.at[(1 - par) * 4 + (y + 4 - k) % 4], base + 3 + k)

    sub = pl.ds(pl.multiple_of(j * 128, 128), 128)

    w_take(1)
    w_take(2)
    s_take(0)
    s_take(1)
    w_take(3)
    w_take(4)
    w_relay(0)
    w_relay(1)
    s_take(2)
    chosen = sp[q, 0, :, sub].astype(F32)
    for zi in range(1, 4):
        chosen = jnp.where(p == zi, sp[q, zi, :, sub].astype(F32), chosen)
    psp[slot] = chosen.astype(BF)
    panel_send(psp, SEM["ps"])
    w_take(5)
    w_take(6)
    w_relay(2)
    w_relay(3)
    s_cross(0, 0)
    s_cross(0, 1)
    s_cross(1, 0)
    s_cross(1, 1)
    w_take(7)
    for d in range(1, Z):
        arrived(eg.at[y, (z + d) % Z], SEM["ez"] + Z - d)
    for k in range(1, Y):
        send(eg.at[y], eg.at[y], SEM["ey"] + k, at_y(k))
    w_relay(4)
    w_relay(5)
    panel_pass(psp, SEM["ps"])
    s_cross(0, 2)
    s_cross(1, 2)
    s_cross(2, 0)
    s_cross(2, 1)
    s_cross(2, 2)
    w_relay(6)
    w_relay(7)

    panel_wait(psp, SEM["ps"])

    def gram_start(g, rows_of, panel_rows):
        rhs = panel_rows
        theirs = lax.dot_general(rows_of(1 - c), rhs, CONTRACT, preferred_element_type=F32)
        gsend[g] = theirs.astype(BF)
        send(gsend.at[g], grecv.at[g], SEM["gc"] + g, (wide, sib))
        gkeep[g] = lax.dot_general(rows_of(c), rhs, CONTRACT, preferred_element_type=F32)

    def spin_rows(cc):
        return jnp.concatenate(
            [
                sp[q, zi, pl.ds(pl.multiple_of((2 * xx + cc) * 16, 16), 16), sub]
                for xx in range(X)
                for zi in range(4)
            ],
            axis=0,
        )

    gram_start(0, spin_rows, psp[...].reshape(PANEL_ROWS, 128))

    for k in range(1, Y):
        arrived(eg.at[(y + 4 - k) % 4], SEM["ey"] + k)
    mean = jnp.sum(jnp.sum(eg[...].reshape(32, 128), axis=0, keepdims=True), axis=1, keepdims=True) / SAMPLES
    shifted = jnp.concatenate([eg[yy, 2 * p + zp] for zp in range(2) for yy in range(Y)], axis=1) - mean
    high = shifted.astype(BF).astype(F32)
    rest = shifted - high
    middle = rest.astype(BF).astype(F32)
    low = rest - middle
    row = lax.broadcasted_iota(jnp.int32, (16, PANEL_ROWS), 0)
    pieces = jnp.where(row == 0, high, jnp.where(row == 1, middle, jnp.where(row == 2, low, 0.0)))
    load_d.wait()
    solved = jnp.sum(
        lax.dot_general(pieces.astype(BF), dg[...], CONTRACT, preferred_element_type=F32), axis=0, keepdims=True
    )

    for t in range(3):
        for k in range(4):
            source = ((x + (0, 3, 1, 2)[k]) % X) * C + (1 - c)
            arrived(sp.at[source, zi_of(t)], sc + 3 * k + t)
    total = None
    for i in range(Z):
        z1 = (z + NEAR[i]) % Z
        if i % 2 == 0:
            arrived(wg.at[z1 * Y + (y + 1) % Y], SEM["wy"] + 8 + i)
        else:
            arrived(wg.at[z1 * Y + (y + 3) % Y], SEM["wy"] + i)
        arrived(wg.at[z1 * Y + (y + 2) % Y], SEM["wy"] + 16 + i)
        term = jnp.dot(
            sp[z1].reshape(512, 512), wg[pl.ds(z1 * Y, Y)].reshape(512, 256), preferred_element_type=F32
        )
        total = term if total is None else total + term
    mine = bias[:, pl.ds(pl.multiple_of(j * 256, 256), 256)]
    fields = jnp.tanh(total + mine).astype(BF)
    f5[...] = fields.reshape(4, X, C, 16, 256)
    pf[slot] = f5[p].reshape(128, 256)
    panel_send(pf, SEM["pf"])
    ft[...] = fields.astype(F32).T

    def gram_x(g):
        arrived(grecv.at[g], SEM["gc"] + g)
        for k in (1, 3, 2):
            rows = pl.ds(pl.multiple_of(((x + k) % X) * 64, 64), 64)
            xsend[g, k] = (gkeep[g, rows, :] + grecv[g, rows, :].astype(F32)).astype(BF)
            send(xsend.at[g, k], xrecv.at[g, k], SEM["gx"] + 4 * g + k, at_x(k))

    def gram_z(g):
        rows = pl.ds(pl.multiple_of(x * 64, 64), 64)
        value = gkeep[g, rows, :] + grecv[g, rows, :].astype(F32)
        for k in (1, 3, 2):
            arrived(xrecv.at[g, k], SEM["gx"] + 4 * g + k)
            value = value + xrecv[g, k].astype(F32)
        tsum[g] = value.reshape(4, 16, PANEL_ROWS)
        for k in (1, 3, 2):
            zi = (j + k) % 4
            zsend[g, k] = tsum[g, zi].astype(BF)
            send(zsend.at[g, k], zrecv.at[g, k], SEM["gz"] + 4 * g + k, at_z(2 * zi + par))

    def gram_end(g):
        value = tsum[g, j]
        for k in (1, 3, 2):
            arrived(zrecv.at[g, k], SEM["gz"] + 4 * g + k)
            value = value + zrecv[g, k].astype(F32)
        return value

    gram_x(0)
    panel_pass(pf, SEM["pf"])
    gram_z(0)
    panel_wait(pf, SEM["pf"])

    def field_rows(cc):
        return jnp.concatenate([f5[zi, xx, cc] for xx in range(X) for zi in range(4)], axis=0)

    gram_start(1, field_rows, pf[...].reshape(PANEL_ROWS, 256))
    gram_x(1)
    spin_total = gram_end(0)
    gram_z(1)
    field_total = gram_end(1)
    gram_column = (spin_total / SPIN_SITES * (field_total / HIDDEN_UNITS)).astype(BF)
    factor = lax.dot_general(gram_column, dg[...], CONTRACT, preferred_element_type=F32)
    factor_out[...] = factor.astype(BF)

    sample = lax.broadcasted_iota(jnp.int32, (16, PANEL_ROWS), 0)
    column = lax.broadcasted_iota(jnp.int32, (16, PANEL_ROWS), 1)
    picked = jnp.sum(
        jnp.where(column == slot * 128 + q * 16 + sample, solved, 0.0), axis=1, keepdims=True
    )
    carried = jnp.sum(factor * solved, axis=1, keepdims=True)
    narrow_row = lax.broadcasted_iota(jnp.int32, (16, 128), 0)
    narrow_col = lax.broadcasted_iota(jnp.int32, (16, 128), 1)
    here = narrow_col == q * 16 + narrow_row
    own = jnp.sum(jnp.where(here, energy[...], 0.0), axis=1, keepdims=True)
    in_panel = jnp.broadcast_to(p, (16, 1)) == j
    update = jnp.where(in_panel, picked, own - mean - carried)
    update_out[...] = jnp.sum(
        jnp.where(narrow_row == narrow_col, update, 0.0), axis=0, keepdims=True
    )
    u1[q] = jnp.sum(jnp.where(here, update, 0.0), axis=0, keepdims=True)
    for d in range(1, Q):
        send(u1.at[q], u1.at[q], SEM["uq"] + d, (wide, (q + d) % Q))
    for d in range(1, Q):
        arrived(u1.at[(q + Q - d) % Q], SEM["uq"] + d)
    u2[j] = jnp.sum(u1[...].reshape(Q, 128), axis=0, keepdims=True)
    for k in (1, 3, 2):
        send(u2.at[j], u2.at[j], SEM["uz"] + k, at_z(2 * ((j + k) % 4) + par))
    for k in (1, 3, 2):
        arrived(u2.at[(j + 4 - k) % 4], SEM["uz"] + k)
    coefficient = jnp.concatenate([u2[zi] for zi in range(4)], axis=1)
    wt[...] = (ft[...] * coefficient).astype(BF)

    def plain(i):
        if i % 2 == 0:
            send(pb.at[i, (y + 3) % Y], r2.at[1, i], SEM["r2"] + 8 + i, at_y(3))
        else:
            send(pb.at[i, (y + 1) % Y], r2.at[0, i], SEM["r2"] + i, at_y(1))

    def combine(i):
        arrived(r1.at[i], SEM["r1"] + i)
        k = 1 if i % 2 == 0 else 3
        qb[i] = (pb[i, (y + k) % Y].astype(F32) + r1[i].astype(F32)).astype(BF)
        if i % 2 == 0:
            send(qb.at[i], r2.at[0, i], SEM["r2"] + i, at_y(1))
        else:
            send(qb.at[i], r2.at[1, i], SEM["r2"] + 8 + i, at_y(3))

    def finish(i):
        z1 = (z + FAR[i]) % Z
        arrived(r2.at[0, i], SEM["r2"] + i)
        arrived(r2.at[1, i], SEM["r2"] + 8 + i)
        value = (pb[i, y].astype(F32) + r2[0, i].astype(F32) + r2[1, i].astype(F32)).astype(BF)
        if FAR[i] == 0:
            r3[z] = value
        else:
            zb[i] = value
            send(zb.at[i], r3.at[z], SEM["r3"] + FAR[i], at_z(z1))

    for i in range(Z):
        z1 = (z + FAR[i]) % Z
        product = jnp.dot(wt[...], sp[z1].reshape(512, 512), preferred_element_type=F32).astype(BF)
        for yy in range(Y):
            pb[i, yy] = product[:, yy * 128 : (yy + 1) * 128]
        send(pb.at[i, (y + 2) % Y], r1.at[i], SEM["r1"] + i, at_y(1 if i % 2 == 0 else 3))
        if i >= 2:
            plain(i - 2)
        if i >= 4:
            combine(i - 4)
    plain(6)
    plain(7)
    for i in range(4, Z):
        combine(i)
        finish(i - 4)
    for i in range(4, Z):
        finish(i)
    for d in range(1, Z):
        arrived(r3.at[(z + d) % Z], SEM["r3"] + Z - d)
    for jj in range(4):
        block = r3[2 * jj].astype(F32) + r3[2 * jj + 1].astype(F32)
        grad_out[:, jj * 256 : (jj + 1) * 256] = block.T / math.sqrt(SAMPLES)
    for copy in sends:
        copy.wait_send()


def local(spins, weights, field_bias, energies, panel_index, diag_inverse):
    vmem = pl.BlockSpec(memory_space=pltpu.VMEM)
    anywhere = pl.BlockSpec(memory_space=pl.ANY)
    smem = pl.BlockSpec(memory_space=pltpu.SMEM)
    grad_w, factor, update = pl.pallas_call(
        kernel,
        out_shape=(
            jax.ShapeDtypeStruct((128, 1024), F32),
            jax.ShapeDtypeStruct((16, PANEL_ROWS), BF),
            jax.ShapeDtypeStruct((1, 128), F32),
        ),
        in_specs=[anywhere, anywhere, vmem, vmem, smem, anywhere],
        out_specs=(vmem, vmem, vmem),
        scratch_shapes=[
            pltpu.VMEM((Q, 128, 512), jnp.int32),
            pltpu.VMEM((Q, 4, 128, 512), BF),
            pltpu.VMEM((32, 128, 256), BF),
            pltpu.VMEM((PANEL_ROWS, PANEL_ROWS), BF),
            pltpu.VMEM((4, X, C, 16, 256), BF),
            pltpu.VMEM((256, 512), F32),
            pltpu.VMEM((Y, Z, 1, 128), F32),
            pltpu.VMEM((8, 128, 128), BF),
            pltpu.VMEM((8, 128, 256), BF),
            pltpu.VMEM((2, 256, PANEL_ROWS), BF),
            pltpu.VMEM((2, 256, PANEL_ROWS), F32),
            pltpu.VMEM((2, 256, PANEL_ROWS), BF),
            pltpu.VMEM((2, 4, 64, PANEL_ROWS), BF),
            pltpu.VMEM((2, 4, 64, PANEL_ROWS), BF),
            pltpu.VMEM((2, 4, 16, PANEL_ROWS), F32),
            pltpu.VMEM((2, 4, 16, PANEL_ROWS), BF),
            pltpu.VMEM((2, 4, 16, PANEL_ROWS), BF),
            pltpu.VMEM((Q, 1, 128), F32),
            pltpu.VMEM((4, 1, 128), F32),
            pltpu.VMEM((256, 512), BF),
            pltpu.VMEM((Z, Y, 256, 128), BF),
            pltpu.VMEM((Z, 256, 128), BF),
            pltpu.VMEM((Z, 256, 128), BF),
            pltpu.VMEM((2, Z, 256, 128), BF),
            pltpu.VMEM((Z, 256, 128), BF),
            pltpu.VMEM((Z, 256, 128), BF),
            pltpu.SemaphoreType.DMA((NSEM,)),
            pltpu.SemaphoreType.DMA((NSEM,)),
            pltpu.SemaphoreType.DMA((10,)),
        ],
        compiler_params=pltpu.CompilerParams(
            collective_id=0, has_side_effects=True, vmem_limit_bytes=56 * 1024 * 1024
        ),
    )(
        spins,
        weights,
        field_bias.reshape(1, -1),
        energies.astype(F32).reshape(1, -1),
        panel_index,
        diag_inverse,
    )
    return grad_w, factor, update[0, :16]


def solution(mesh):
    in_specs = (P("wide", None), P("wide", "narrow"), P("narrow"), P("wide"), P(), P())
    out_specs = (P("wide", "narrow"), P(("wide", "narrow"), None), P(("wide", "narrow")))
    return jax.shard_map(local, mesh=mesh, in_specs=in_specs, out_specs=out_specs, check_vma=False)
```

```python
import functools
import math

import jax
import jax.numpy as jnp
from jax import lax
from jax.experimental import pallas as pl
from jax.experimental.pallas import tpu as pltpu
from jax.sharding import PartitionSpec as P

SPIN_SITES = 4096
HIDDEN_UNITS = 8192
PANEL_ROWS = 1024
SAMPLES = 4096
Z, Y, X, C = 8, 4, 4, 2
Q = X * C
NEAR = (0, 1, -1, -2, 2, -3, 3, 4)
FAR = (4, 3, 5, 2, 6, 1, 7, 0)
SAME = (2, 6, 4)
UNITS = ((0, 0), (1, 1), (0, 1), (1, 0), (2, 0), (2, 1))
MESH = pl.DeviceIdType.MESH
BF = jnp.bfloat16
F32 = jnp.float32
CONTRACT = (((1,), (1,)), ((), ()))


class Sems:
    def __init__(self):
        self.n = 0

    def take(self, n):
        self.n += n
        return self.n - n


def layout():
    s = Sems()
    names = dict(
        wz=8, wy=24, sz=6, sx=18, sc=24, ty=4, tx=18, tc=24, ez=8, ey=4, ps=7, pf=7, fy=4,
        gc=2, gx=8, gz=8, uq=8, up=16, r3=8,
    )
    return {k: s.take(n) for k, n in names.items()}, s.n


SEM, NSEM = layout()


def kernel(
    spins, weights, bias, energy, panel, diag,
    grad_out, factor_out, update_out,
    s32, sp, wg, dg, f5, eg, psp, pf,
    gsend, gkeep, grecv, xsend, xrecv, tsum, zsend, zrecv,
    u1, u2, wt, s2, fty, zb, r3,
    ssem, rsem, lsem,
):
    wide = lax.axis_index("wide")
    q = lax.axis_index("narrow")
    z, y = wide // Y, wide % Y
    x, c = q // C, q % C
    par, j = z % 2, z // 2
    sib = x * C + (1 - c)
    sign = 1 - 2 * par
    partner = z + sign
    sends = []

    def at_z(zz):
        return (zz * Y + y, q)

    def at_y(k):
        return (z * Y + (y + k) % Y, q)

    def at_x(k):
        return (wide, ((x + k) % X) * C + c)

    def send(src, dst, index, device):
        copy = pltpu.make_async_remote_copy(
            src_ref=src, dst_ref=dst, send_sem=ssem.at[index], recv_sem=rsem.at[index],
            device_id=device, device_id_type=MESH,
        )
        copy.start()
        sends.append(copy)

    def arrived(dst, index):
        pltpu.make_async_remote_copy(
            src_ref=dst, dst_ref=dst, send_sem=ssem.at[index], recv_sem=rsem.at[index],
            device_id=(wide, sib), device_id_type=MESH,
        ).wait_recv()

    def load_spins(k):
        return pltpu.make_async_copy(spins.at[:, pl.ds(pl.multiple_of(k * 512, 512), 512)], s32.at[k], lsem.at[k])

    for d in range(Q):
        load_spins((q + d) % Q).start()
    my_w = weights.at[:, pl.ds(pl.multiple_of(j * 256, 256), 256)]
    load_w = pltpu.make_async_copy(my_w, wg.at[wide], lsem.at[8])
    load_w.start()
    load_d = pltpu.make_async_copy(diag, dg, lsem.at[9])
    load_d.start()

    barrier = pltpu.get_barrier_semaphore()
    for d in range(1, Z):
        pl.semaphore_signal(barrier, inc=1, device_id=at_z((z + d) % Z), device_id_type=MESH)
    for k in range(1, Y):
        pl.semaphore_signal(barrier, inc=1, device_id=at_y(k), device_id_type=MESH)
    for d in range(1, Q):
        pl.semaphore_signal(barrier, inc=1, device_id=(wide, (q + d) % Q), device_id_type=MESH)

    def convert(k):
        load_spins(k).wait()
        sp[k, j] = s32[k].astype(F32).astype(BF)

    convert(q)
    eg[y, z] = energy[...]
    load_w.wait()
    pl.semaphore_wait(barrier, Z + Y + Q - 3)

    def w_y(i, z1):
        chunk = wg.at[z1 * Y + y]
        send(chunk, chunk, SEM["wy"] + i, at_y(1))
        send(chunk, chunk, SEM["wy"] + 8 + i, at_y(-1 + Y))

    def toward(o):
        return (z + sign * o + Z) % Z

    def w_z(o):
        zd = toward(o)
        src = weights.at[:, pl.ds(pl.multiple_of((zd // 2) * 256, 256), 256)]
        seen = {1: 1, -1: -1, 2: -2, -3: -3}[o]
        send(src, wg.at[wide], SEM["wz"] + 3 + seen, at_z(zd))

    def s_z(u):
        t, h = UNITS[u]
        mine = sp.at[q, j, pl.ds(64 * h, 64)]
        send(mine, mine, SEM["sz"] + u, at_z((z + (6, 2)[t]) % Z))

    w_y(0, z)
    s_z(0)
    s_z(1)
    w_z(1)
    w_z(-1)
    s_z(2)
    s_z(3)
    w_z(2)
    w_z(-3)
    for d in range(1, Z):
        send(eg.at[y, z], eg.at[y, z], SEM["ez"] + d, at_z((z + d) % Z))
    for d in range(1, Q):
        convert((q + d) % Q)

    def w_take(i):
        o = NEAR[i]
        z1 = toward(o)
        chunk = wg.at[z1 * Y + y]
        arrived(chunk, SEM["wz"] + 3 + o)
        if o < 0:
            send(chunk, chunk, SEM["wz"] + 4 - o, at_z(partner))
        w_y(i, z1)

    def w_relay(i):
        z1 = toward(NEAR[i])
        if i % 2 == 0:
            chunk = wg.at[z1 * Y + (y + 3) % Y]
            arrived(chunk, SEM["wy"] + i)
            send(chunk, chunk, SEM["wy"] + 16 + i, at_y(1))
        else:
            chunk = wg.at[z1 * Y + (y + 1) % Y]
            arrived(chunk, SEM["wy"] + 8 + i)
            send(chunk, chunk, SEM["wy"] + 16 + i, at_y(3))

    def zi_of(t):
        return ((z + SAME[t]) % Z) // 2

    def s_piece(source, u):
        t, h = UNITS[u]
        return sp.at[source, zi_of(t), pl.ds(64 * h, 64)]

    def s_arrive(u):
        got = s_piece(q, u)
        arrived(got, SEM["sz"] + u)
        if u < 2:
            send(got, got, SEM["sz"] + 4 + u, at_z((z + (6, 2)[u]) % Z))

    def spread(piece, bx, bc):
        def begin(u):
            mine = piece(q, u)
            send(mine, mine, bx + u, at_x(1))
            send(mine, mine, bx + 6 + u, at_x(3))
            send(mine, mine, bc + u, (wide, sib))

        def cross(u, k):
            source = ((x + (3, 1, 2)[k]) % X) * C + c
            got = piece(source, u)
            arrived(got, bx + 6 * k + u)
            if k == u % 2:
                send(got, got, bx + 12 + u, at_x((1, 3)[k]))
            send(got, got, bc + 6 * (k + 1) + u, (wide, sib))

        def end(u):
            for k in range(4):
                source = ((x + (0, 3, 1, 2)[k]) % X) * C + (1 - c)
                arrived(piece(source, u), bc + 6 * k + u)

        return begin, cross, end

    s_begin, s_cross, s_end = spread(s_piece, SEM["sx"], SEM["sc"])
    t_begin, t_cross, t_end = spread(
        lambda source, u: s2.at[source, (y + u // 2 + 1) % Y, pl.ds(2 * (u % 2), 2)], SEM["tx"], SEM["tc"]
    )

    def t_send(k):
        columns = pl.ds(pl.multiple_of(((y + k) % Y) * 128, 128), 128)
        send(sp.at[q, :, :, columns], s2.at[q, y], SEM["ty"] + k, at_y(k))

    def t_arrive(t):
        arrived(s2.at[q, (y + t + 1) % Y], SEM["ty"] + Y - 1 - t)

    p = panel[0]
    slot = par * 4 + y
    other = (1 - par) * 4 + y

    def panel_send(buf, base):
        send(buf.at[slot], buf.at[slot], base, at_z(partner))
        for k in (1, 3, 2):
            send(buf.at[slot], buf.at[slot], base + k, at_y(k))

    def panel_pass(buf, base):
        arrived(buf.at[other], base)
        for k in (1, 3, 2):
            send(buf.at[other], buf.at[other], base + 3 + k, at_y(k))

    def panel_wait(buf, base):
        for k in (1, 3, 2):
            arrived(buf.at[par * 4 + (y + 4 - k) % 4], base + k)
            arrived(buf.at[(1 - par) * 4 + (y + 4 - k) % 4], base + 3 + k)

    sub = pl.ds(pl.multiple_of(j * 128, 128), 128)

    s_arrive(0)
    s_begin(0)
    s_arrive(1)
    s_begin(1)
    w_take(1)
    w_take(2)
    s_arrive(2)
    s_begin(2)
    s_arrive(3)
    s_begin(3)
    w_relay(0)
    s_cross(0, 0)
    s_cross(0, 1)
    s_cross(1, 0)
    s_cross(1, 1)
    w_take(3)
    w_relay(1)
    s_arrive(4)
    s_begin(4)
    s_arrive(5)
    s_begin(5)
    w_relay(2)
    chosen = sp[q, 0, :, sub].astype(F32)
    for zi in range(1, 4):
        chosen = jnp.where(p == zi, sp[q, zi, :, sub].astype(F32), chosen)
    psp[slot] = chosen.astype(BF)
    panel_send(psp, SEM["ps"])
    s_cross(2, 0)
    s_cross(2, 1)
    s_cross(3, 0)
    s_cross(3, 1)
    w_take(4)
    w_relay(3)
    w_take(5)
    w_take(6)
    w_relay(4)
    s_cross(0, 2)
    s_cross(1, 2)
    s_cross(2, 2)
    s_cross(3, 2)
    s_cross(4, 0)
    s_cross(4, 1)
    s_cross(5, 0)
    s_cross(5, 1)
    w_take(7)
    w_relay(5)
    panel_pass(psp, SEM["ps"])
    for d in range(1, Z):
        arrived(eg.at[y, (z + d) % Z], SEM["ez"] + Z - d)
    for k in range(1, Y):
        send(eg.at[y], eg.at[y], SEM["ey"] + k, at_y(k))
    w_relay(6)
    w_relay(7)
    s_cross(4, 2)
    s_cross(5, 2)
    for k in (1, 3, 2):
        t_send(k)

    panel_wait(psp, SEM["ps"])

    def gram_start(g, rows_of, panel_rows):
        rhs = panel_rows
        theirs = lax.dot_general(rows_of(1 - c), rhs, CONTRACT, preferred_element_type=F32)
        gsend[g] = theirs.astype(BF)
        send(gsend.at[g], grecv.at[g], SEM["gc"] + g, (wide, sib))
        gkeep[g] = lax.dot_general(rows_of(c), rhs, CONTRACT, preferred_element_type=F32)

    def spin_rows(cc):
        return jnp.concatenate(
            [
                sp[q, zi, pl.ds(pl.multiple_of((2 * xx + cc) * 16, 16), 16), sub]
                for xx in range(X)
                for zi in range(4)
            ],
            axis=0,
        )

    gram_start(0, spin_rows, psp[...].reshape(PANEL_ROWS, 128))

    for k in range(1, Y):
        arrived(eg.at[(y + 4 - k) % 4], SEM["ey"] + k)
    mean = jnp.sum(jnp.sum(eg[...].reshape(32, 128), axis=0, keepdims=True), axis=1, keepdims=True) / SAMPLES
    shifted = jnp.concatenate([eg[yy, 2 * p + zp] for zp in range(2) for yy in range(Y)], axis=1) - mean
    high = shifted.astype(BF).astype(F32)
    rest = shifted - high
    middle = rest.astype(BF).astype(F32)
    low = rest - middle
    row = lax.broadcasted_iota(jnp.int32, (16, PANEL_ROWS), 0)
    pieces = jnp.where(row == 0, high, jnp.where(row == 1, middle, jnp.where(row == 2, low, 0.0)))
    load_d.wait()
    solved = jnp.sum(
        lax.dot_general(pieces.astype(BF), dg[...], CONTRACT, preferred_element_type=F32), axis=0, keepdims=True
    )

    for u in range(6):
        s_end(u)
    total = None
    for i in range(Z):
        z1 = toward(NEAR[i])
        if i % 2 == 0:
            arrived(wg.at[z1 * Y + (y + 1) % Y], SEM["wy"] + 8 + i)
        else:
            arrived(wg.at[z1 * Y + (y + 3) % Y], SEM["wy"] + i)
        arrived(wg.at[z1 * Y + (y + 2) % Y], SEM["wy"] + 16 + i)
        term = jnp.dot(
            sp[z1].reshape(512, 512), wg[pl.ds(z1 * Y, Y)].reshape(512, 256), preferred_element_type=F32
        )
        total = term if total is None else total + term
    mine = bias[:, pl.ds(pl.multiple_of(j * 256, 256), 256)]
    fields = jnp.tanh(total + mine).astype(BF)
    f5[...] = fields.reshape(4, X, C, 16, 256)
    pf[slot] = f5[p].reshape(128, 256)
    panel_send(pf, SEM["pf"])

    def gram_x(g):
        arrived(grecv.at[g], SEM["gc"] + g)
        for k in (1, 3, 2):
            rows = pl.ds(pl.multiple_of(((x + k) % X) * 64, 64), 64)
            xsend[g, k] = (gkeep[g, rows, :] + grecv[g, rows, :].astype(F32)).astype(BF)
            send(xsend.at[g, k], xrecv.at[g, k], SEM["gx"] + 4 * g + k, at_x(k))

    def gram_z(g):
        rows = pl.ds(pl.multiple_of(x * 64, 64), 64)
        value = gkeep[g, rows, :] + grecv[g, rows, :].astype(F32)
        for k in (1, 3, 2):
            arrived(xrecv.at[g, k], SEM["gx"] + 4 * g + k)
            value = value + xrecv[g, k].astype(F32)
        tsum[g] = value.reshape(4, 16, PANEL_ROWS)
        for k in (1, 3, 2):
            zi = (j + k) % 4
            zsend[g, k] = tsum[g, zi].astype(BF)
            send(zsend.at[g, k], zrecv.at[g, k], SEM["gz"] + 4 * g + k, at_z(2 * zi + par))

    def gram_end(g):
        value = tsum[g, j]
        for k in (1, 3, 2):
            arrived(zrecv.at[g, k], SEM["gz"] + 4 * g + k)
            value = value + zrecv[g, k].astype(F32)
        return value

    gram_x(0)
    for t in (0, 2):
        t_arrive(t)
        t_begin(2 * t)
        t_begin(2 * t + 1)
    fty[y] = fields.astype(F32).T.astype(BF)
    panel_pass(pf, SEM["pf"])
    send(fty.at[y], fty.at[y], SEM["fy"], at_y(1))
    send(fty.at[y], fty.at[y], SEM["fy"] + 1, at_y(3))
    gram_z(0)
    panel_wait(pf, SEM["pf"])

    def field_rows(cc):
        return jnp.concatenate([f5[zi, xx, cc] for xx in range(X) for zi in range(4)], axis=0)

    gram_start(1, field_rows, pf[...].reshape(PANEL_ROWS, 256))
    gram_x(1)
    t_arrive(1)
    t_begin(2)
    t_begin(3)
    for u in (0, 1, 4, 5):
        t_cross(u, 0)
        t_cross(u, 1)
    gram_z(1)
    for k in range(2):
        passed = fty.at[(y + (3, 1)[k]) % Y]
        arrived(passed, SEM["fy"] + k)
        part = fty.at[(y + (3, 1)[k]) % Y, pl.ds(128 * k, 128)]
        send(part, part, SEM["fy"] + 2 + k, at_y((1, 3)[k]))
    spin_total = gram_end(0)
    for u in (2, 3):
        t_cross(u, 0)
        t_cross(u, 1)
    field_total = gram_end(1)
    gram_column = (spin_total / SPIN_SITES * (field_total / HIDDEN_UNITS)).astype(BF)
    factor = lax.dot_general(gram_column, dg[...], CONTRACT, preferred_element_type=F32)
    factor_out[...] = factor.astype(BF)

    sample = lax.broadcasted_iota(jnp.int32, (16, PANEL_ROWS), 0)
    column = lax.broadcasted_iota(jnp.int32, (16, PANEL_ROWS), 1)
    picked = jnp.sum(
        jnp.where(column == slot * 128 + q * 16 + sample, solved, 0.0), axis=1, keepdims=True
    )
    carried = jnp.sum(factor * solved, axis=1, keepdims=True)
    narrow_row = lax.broadcasted_iota(jnp.int32, (16, 128), 0)
    narrow_col = lax.broadcasted_iota(jnp.int32, (16, 128), 1)
    here = narrow_col == q * 16 + narrow_row
    own = jnp.sum(jnp.where(here, energy[...], 0.0), axis=1, keepdims=True)
    in_panel = jnp.broadcast_to(p, (16, 1)) == j
    update = jnp.where(in_panel, picked, own - mean - carried)
    update_out[...] = jnp.sum(
        jnp.where(narrow_row == narrow_col, update, 0.0), axis=0, keepdims=True
    )
    u1[q] = jnp.sum(jnp.where(here, update, 0.0), axis=0, keepdims=True)
    for d in range(1, Q):
        send(u1.at[q], u1.at[q], SEM["uq"] + d, (wide, (q + d) % Q))
    for d in range(1, Q):
        arrived(u1.at[(q + Q - d) % Q], SEM["uq"] + d)
    u2[y, j] = jnp.sum(u1[...].reshape(Q, 128), axis=0, keepdims=True)
    plane = [(kz, ky) for kz in (0, 1, 3, 2) for ky in (0, 1, 3, 2)][1:]
    for kz, ky in plane:
        device = ((2 * ((j + kz) % 4) + par) * Y + (y + ky) % Y, q)
        send(u2.at[y, j], u2.at[y, j], SEM["up"] + 4 * kz + ky, device)
    for u in range(6):
        t_cross(u, 2)
    for u in range(6):
        t_end(u)
    for k in range(2):
        arrived(fty.at[(y + 2) % Y, pl.ds(128 * k, 128)], SEM["fy"] + 2 + k)
    for kz, ky in plane:
        arrived(u2.at[(y + 4 - ky) % Y, (j + 4 - kz) % 4], SEM["up"] + 4 * kz + ky)
    for yy in range(Y):
        coefficient = jnp.concatenate([u2[yy, zi] for zi in range(4)], axis=1)
        wt[yy] = (fty[yy].astype(F32) * coefficient).astype(BF)

    mine_y = pl.ds(pl.multiple_of(y * 128, 128), 128)

    def sites(i, k):
        z1 = (z + FAR[i]) % Z
        if k == 0:
            return sp[z1, :, :, mine_y].reshape(512, 128)
        return s2[z1, (y + k) % Y].reshape(512, 128)

    for i in range(0, Z, 2):
        product = None
        for k in range(Y):
            both = jnp.concatenate([sites(i, k), sites(i + 1, k)], axis=1)
            term = jnp.dot(wt[(y + k) % Y], both, preferred_element_type=F32)
            product = term if product is None else product + term
        for n in range(2):
            value = product[:, n * 128 : (n + 1) * 128].astype(BF)
            off = FAR[i + n]
            if off == 0:
                r3[z] = value
            else:
                zb[i + n] = value
                send(zb.at[i + n], r3.at[z], SEM["r3"] + off, at_z((z + off) % Z))
    for d in range(1, Z):
        arrived(r3.at[(z + d) % Z], SEM["r3"] + Z - d)
    for jj in range(4):
        block = r3[2 * jj].astype(F32) + r3[2 * jj + 1].astype(F32)
        grad_out[:, jj * 256 : (jj + 1) * 256] = block.T / math.sqrt(SAMPLES)
    for copy in sends:
        copy.wait_send()


def local(spins, weights, field_bias, energies, panel_index, diag_inverse):
    vmem = pl.BlockSpec(memory_space=pltpu.VMEM)
    anywhere = pl.BlockSpec(memory_space=pl.ANY)
    smem = pl.BlockSpec(memory_space=pltpu.SMEM)
    grad_w, factor, update = pl.pallas_call(
        kernel,
        out_shape=(
            jax.ShapeDtypeStruct((128, 1024), F32),
            jax.ShapeDtypeStruct((16, PANEL_ROWS), BF),
            jax.ShapeDtypeStruct((1, 128), F32),
        ),
        in_specs=[anywhere, anywhere, vmem, vmem, smem, anywhere],
        out_specs=(vmem, vmem, vmem),
        scratch_shapes=[
            pltpu.VMEM((Q, 128, 512), jnp.int32),
            pltpu.VMEM((Q, 4, 128, 512), BF),
            pltpu.VMEM((32, 128, 256), BF),
            pltpu.VMEM((PANEL_ROWS, PANEL_ROWS), BF),
            pltpu.VMEM((4, X, C, 16, 256), BF),
            pltpu.VMEM((Y, Z, 1, 128), F32),
            pltpu.VMEM((8, 128, 128), BF),
            pltpu.VMEM((8, 128, 256), BF),
            pltpu.VMEM((2, 256, PANEL_ROWS), BF),
            pltpu.VMEM((2, 256, PANEL_ROWS), F32),
            pltpu.VMEM((2, 256, PANEL_ROWS), BF),
            pltpu.VMEM((2, 4, 64, PANEL_ROWS), BF),
            pltpu.VMEM((2, 4, 64, PANEL_ROWS), BF),
            pltpu.VMEM((2, 4, 16, PANEL_ROWS), F32),
            pltpu.VMEM((2, 4, 16, PANEL_ROWS), BF),
            pltpu.VMEM((2, 4, 16, PANEL_ROWS), BF),
            pltpu.VMEM((Q, 1, 128), F32),
            pltpu.VMEM((Y, 4, 1, 128), F32),
            pltpu.VMEM((Y, 256, 512), BF),
            pltpu.VMEM((Q, Y, 4, 128, 128), BF),
            pltpu.VMEM((Y, 256, 512), BF),
            pltpu.VMEM((Z, 256, 128), BF),
            pltpu.VMEM((Z, 256, 128), BF),
            pltpu.SemaphoreType.DMA((NSEM,)),
            pltpu.SemaphoreType.DMA((NSEM,)),
            pltpu.SemaphoreType.DMA((10,)),
        ],
        compiler_params=pltpu.CompilerParams(
            collective_id=0, has_side_effects=True, vmem_limit_bytes=56 * 1024 * 1024
        ),
    )(
        spins,
        weights,
        field_bias.reshape(1, -1),
        energies.astype(F32).reshape(1, -1),
        panel_index,
        diag_inverse,
    )
    return grad_w, factor, update[0, :16]


def solution(mesh):
    in_specs = (P("wide", None), P("wide", "narrow"), P("narrow"), P("wide"), P(), P())
    out_specs = (P("wide", "narrow"), P(("wide", "narrow"), None), P(("wide", "narrow")))
    return jax.shard_map(local, mesh=mesh, in_specs=in_specs, out_specs=out_specs, check_vma=False)
```

```python
import functools
import math

import jax
import jax.numpy as jnp
from jax import lax
from jax.experimental import pallas as pl
from jax.experimental.pallas import tpu as pltpu
from jax.sharding import PartitionSpec as P

SPIN_SITES = 4096
HIDDEN_UNITS = 8192
PANEL_ROWS = 1024
SAMPLES = 4096
Z, Y, X, C = 8, 4, 4, 2
Q = X * C
NEAR = (0, 1, -1, -2, 2, -3, 3, 4)
FAR = (4, 3, 5, 2, 6, 1, 7, 0)
SAME = (2, 6, 4)
UNITS = ((0, 0), (1, 1), (0, 1), (1, 0), (2, 0), (2, 1))
MESH = pl.DeviceIdType.MESH
BF = jnp.bfloat16
F32 = jnp.float32
CONTRACT = (((1,), (1,)), ((), ()))


class Sems:
    def __init__(self):
        self.n = 0

    def take(self, n):
        self.n += n
        return self.n - n


def layout():
    s = Sems()
    names = dict(
        wz=8, wy=24, sz=6, sx=18, sc=24, ty=4, tx=18, tc=24, ez=8, ey=4, ps=7, pf=7, fy=4,
        gc=2, gx=8, gz=8, uq=8, up=16, r3=8,
    )
    return {k: s.take(n) for k, n in names.items()}, s.n


SEM, NSEM = layout()


def kernel(
    spins, weights, bias, energy, panel, diag,
    r3, factor_out, update_out,
    s32, sp, wg, dg, f5, eg, psp, pf,
    gsend, gkeep, grecv, xsend, xrecv, tsum, zsend, zrecv,
    u1, u2, wt, s2, fty, zb,
    ssem, rsem, lsem,
):
    wide = lax.axis_index("wide")
    q = lax.axis_index("narrow")
    z, y = wide // Y, wide % Y
    x, c = q // C, q % C
    par, j = z % 2, z // 2
    sib = x * C + (1 - c)
    sign = 1 - 2 * par
    partner = z + sign
    sends = []

    def at_z(zz):
        return (zz * Y + y, q)

    def at_y(k):
        return (z * Y + (y + k) % Y, q)

    def at_x(k):
        return (wide, ((x + k) % X) * C + c)

    def send(src, dst, index, device):
        copy = pltpu.make_async_remote_copy(
            src_ref=src, dst_ref=dst, send_sem=ssem.at[index], recv_sem=rsem.at[index],
            device_id=device, device_id_type=MESH,
        )
        copy.start()
        sends.append(copy)

    def arrived(dst, index):
        pltpu.make_async_remote_copy(
            src_ref=dst, dst_ref=dst, send_sem=ssem.at[index], recv_sem=rsem.at[index],
            device_id=(wide, sib), device_id_type=MESH,
        ).wait_recv()

    def load_spins(k):
        return pltpu.make_async_copy(spins.at[:, pl.ds(pl.multiple_of(k * 512, 512), 512)], s32.at[k], lsem.at[k])

    for d in range(Q):
        load_spins((q + d) % Q).start()
    my_w = weights.at[:, pl.ds(pl.multiple_of(j * 256, 256), 256)]
    load_w = pltpu.make_async_copy(my_w, wg.at[wide], lsem.at[8])
    load_w.start()
    load_d = pltpu.make_async_copy(diag, dg, lsem.at[9])
    load_d.start()

    barrier = pltpu.get_barrier_semaphore()
    for d in range(1, Z):
        pl.semaphore_signal(barrier, inc=1, device_id=at_z((z + d) % Z), device_id_type=MESH)
    for k in range(1, Y):
        pl.semaphore_signal(barrier, inc=1, device_id=at_y(k), device_id_type=MESH)
    for d in range(1, Q):
        pl.semaphore_signal(barrier, inc=1, device_id=(wide, (q + d) % Q), device_id_type=MESH)

    def convert(k):
        load_spins(k).wait()
        sp[k, j] = s32[k].astype(F32).astype(BF)

    convert(q)
    energy_row = energy[...].astype(F32).reshape(1, 128)
    eg[y, z] = energy_row
    load_w.wait()
    pl.semaphore_wait(barrier, Z + Y + Q - 3)

    def w_y(i, z1):
        chunk = wg.at[z1 * Y + y]
        send(chunk, chunk, SEM["wy"] + i, at_y(1))
        send(chunk, chunk, SEM["wy"] + 8 + i, at_y(-1 + Y))

    def toward(o):
        return (z + sign * o + Z) % Z

    def w_z(o):
        zd = toward(o)
        src = weights.at[:, pl.ds(pl.multiple_of((zd // 2) * 256, 256), 256)]
        seen = {1: 1, -1: -1, 2: -2, -3: -3}[o]
        send(src, wg.at[wide], SEM["wz"] + 3 + seen, at_z(zd))

    def s_z(u):
        t, h = UNITS[u]
        mine = sp.at[q, j, pl.ds(64 * h, 64)]
        send(mine, mine, SEM["sz"] + u, at_z((z + (6, 2)[t]) % Z))

    w_y(0, z)
    s_z(0)
    s_z(1)
    w_z(1)
    w_z(-1)
    s_z(2)
    s_z(3)
    w_z(2)
    w_z(-3)
    for d in range(1, Z):
        send(eg.at[y, z], eg.at[y, z], SEM["ez"] + d, at_z((z + d) % Z))
    for d in range(1, Q):
        convert((q + d) % Q)

    def w_take(i):
        o = NEAR[i]
        z1 = toward(o)
        chunk = wg.at[z1 * Y + y]
        arrived(chunk, SEM["wz"] + 3 + o)
        if o < 0:
            send(chunk, chunk, SEM["wz"] + 4 - o, at_z(partner))
        w_y(i, z1)

    def w_relay(i):
        z1 = toward(NEAR[i])
        if i % 2 == 0:
            chunk = wg.at[z1 * Y + (y + 3) % Y]
            arrived(chunk, SEM["wy"] + i)
            send(chunk, chunk, SEM["wy"] + 16 + i, at_y(1))
        else:
            chunk = wg.at[z1 * Y + (y + 1) % Y]
            arrived(chunk, SEM["wy"] + 8 + i)
            send(chunk, chunk, SEM["wy"] + 16 + i, at_y(3))

    def zi_of(t):
        return ((z + SAME[t]) % Z) // 2

    def s_piece(source, u):
        t, h = UNITS[u]
        return sp.at[source, zi_of(t), pl.ds(64 * h, 64)]

    def s_arrive(u):
        got = s_piece(q, u)
        arrived(got, SEM["sz"] + u)
        if u < 2:
            send(got, got, SEM["sz"] + 4 + u, at_z((z + (6, 2)[u]) % Z))

    def spread(piece, bx, bc):
        def begin(u):
            mine = piece(q, u)
            send(mine, mine, bx + u, at_x(1))
            send(mine, mine, bx + 6 + u, at_x(3))
            send(mine, mine, bc + u, (wide, sib))

        def cross(u, k):
            source = ((x + (3, 1, 2)[k]) % X) * C + c
            got = piece(source, u)
            arrived(got, bx + 6 * k + u)
            if k == u % 2:
                send(got, got, bx + 12 + u, at_x((1, 3)[k]))
            send(got, got, bc + 6 * (k + 1) + u, (wide, sib))

        def end(u):
            for k in range(4):
                source = ((x + (0, 3, 1, 2)[k]) % X) * C + (1 - c)
                arrived(piece(source, u), bc + 6 * k + u)

        return begin, cross, end

    s_begin, s_cross, s_end = spread(s_piece, SEM["sx"], SEM["sc"])
    t_begin, t_cross, t_end = spread(
        lambda source, u: s2.at[source, (y + u // 2 + 1) % Y, pl.ds(2 * (u % 2), 2)], SEM["tx"], SEM["tc"]
    )

    def t_send(k):
        columns = pl.ds(pl.multiple_of(((y + k) % Y) * 128, 128), 128)
        send(sp.at[q, :, :, columns], s2.at[q, y], SEM["ty"] + k, at_y(k))

    def t_arrive(t):
        arrived(s2.at[q, (y + t + 1) % Y], SEM["ty"] + Y - 1 - t)

    p = panel[0]
    slot = par * 4 + y
    other = (1 - par) * 4 + y

    def panel_send(buf, base):
        send(buf.at[slot], buf.at[slot], base, at_z(partner))
        for k in (1, 3, 2):
            send(buf.at[slot], buf.at[slot], base + k, at_y(k))

    def panel_pass(buf, base):
        arrived(buf.at[other], base)
        for k in (1, 3, 2):
            send(buf.at[other], buf.at[other], base + 3 + k, at_y(k))

    def panel_wait(buf, base):
        for k in (1, 3, 2):
            arrived(buf.at[par * 4 + (y + 4 - k) % 4], base + k)
            arrived(buf.at[(1 - par) * 4 + (y + 4 - k) % 4], base + 3 + k)

    sub = pl.ds(pl.multiple_of(j * 128, 128), 128)

    s_arrive(0)
    s_begin(0)
    s_arrive(1)
    s_begin(1)
    w_take(1)
    w_take(2)
    s_arrive(2)
    s_begin(2)
    s_arrive(3)
    s_begin(3)
    w_relay(0)
    s_cross(0, 0)
    s_cross(0, 1)
    s_cross(1, 0)
    s_cross(1, 1)
    w_take(3)
    w_relay(1)
    s_arrive(4)
    s_begin(4)
    s_arrive(5)
    s_begin(5)
    w_relay(2)
    chosen = sp[q, 0, :, sub].astype(F32)
    for zi in range(1, 4):
        chosen = jnp.where(p == zi, sp[q, zi, :, sub].astype(F32), chosen)
    psp[slot] = chosen.astype(BF)
    panel_send(psp, SEM["ps"])
    s_cross(2, 0)
    s_cross(2, 1)
    s_cross(3, 0)
    s_cross(3, 1)
    w_take(4)
    w_relay(3)
    w_take(5)
    w_take(6)
    w_relay(4)
    s_cross(0, 2)
    s_cross(1, 2)
    s_cross(2, 2)
    s_cross(3, 2)
    s_cross(4, 0)
    s_cross(4, 1)
    s_cross(5, 0)
    s_cross(5, 1)
    w_take(7)
    w_relay(5)
    panel_pass(psp, SEM["ps"])
    for d in range(1, Z):
        arrived(eg.at[y, (z + d) % Z], SEM["ez"] + Z - d)
    for k in range(1, Y):
        send(eg.at[y], eg.at[y], SEM["ey"] + k, at_y(k))
    w_relay(6)
    w_relay(7)
    s_cross(4, 2)
    s_cross(5, 2)

    def gram_start(g, rows_of, panel_rows):
        rhs = panel_rows
        theirs = lax.dot_general(rows_of(1 - c), rhs, CONTRACT, preferred_element_type=F32)
        gsend[g] = theirs.astype(BF)
        send(gsend.at[g], grecv.at[g], SEM["gc"] + g, (wide, sib))
        gkeep[g] = lax.dot_general(rows_of(c), rhs, CONTRACT, preferred_element_type=F32)

    def spin_rows(cc):
        return jnp.concatenate(
            [
                sp[q, zi, pl.ds(pl.multiple_of((2 * xx + cc) * 16, 16), 16), sub]
                for xx in range(X)
                for zi in range(4)
            ],
            axis=0,
        )

    def gram_x(g):
        arrived(grecv.at[g], SEM["gc"] + g)
        for k in (1, 3, 2):
            rows = pl.ds(pl.multiple_of(((x + k) % X) * 64, 64), 64)
            xsend[g, k] = (gkeep[g, rows, :] + grecv[g, rows, :].astype(F32)).astype(BF)
            send(xsend.at[g, k], xrecv.at[g, k], SEM["gx"] + 4 * g + k, at_x(k))

    def gram_z(g):
        rows = pl.ds(pl.multiple_of(x * 64, 64), 64)
        value = gkeep[g, rows, :] + grecv[g, rows, :].astype(F32)
        for k in (1, 3, 2):
            arrived(xrecv.at[g, k], SEM["gx"] + 4 * g + k)
            value = value + xrecv[g, k].astype(F32)
        tsum[g] = value.reshape(4, 16, PANEL_ROWS)
        for k in (1, 3, 2):
            zi = (j + k) % 4
            zsend[g, k] = tsum[g, zi].astype(BF)
            send(zsend.at[g, k], zrecv.at[g, k], SEM["gz"] + 4 * g + k, at_z(2 * zi + par))

    def gram_end(g):
        value = tsum[g, j]
        for k in (1, 3, 2):
            arrived(zrecv.at[g, k], SEM["gz"] + 4 * g + k)
            value = value + zrecv[g, k].astype(F32)
        return value

    def field_rows(cc):
        return jnp.concatenate([f5[zi, xx, cc] for xx in range(X) for zi in range(4)], axis=0)

    for u in range(6):
        s_end(u)
    total = None
    for i in range(Z):
        z1 = toward(NEAR[i])
        if i % 2 == 0:
            arrived(wg.at[z1 * Y + (y + 1) % Y], SEM["wy"] + 8 + i)
        else:
            arrived(wg.at[z1 * Y + (y + 3) % Y], SEM["wy"] + i)
        arrived(wg.at[z1 * Y + (y + 2) % Y], SEM["wy"] + 16 + i)
        term = jnp.dot(
            sp[z1].reshape(512, 512), wg[pl.ds(z1 * Y, Y)].reshape(512, 256), preferred_element_type=F32
        )
        total = term if total is None else total + term
    mine = bias[:, pl.ds(pl.multiple_of(j * 256, 256), 256)]
    fields = jnp.tanh(total + mine).astype(BF)
    f5[...] = fields.reshape(4, X, C, 16, 256)
    pf[slot] = f5[p].reshape(128, 256)
    panel_send(pf, SEM["pf"])

    panel_wait(psp, SEM["ps"])
    gram_start(0, spin_rows, psp[...].reshape(PANEL_ROWS, 128))
    panel_pass(pf, SEM["pf"])
    for k in (1, 3, 2):
        t_send(k)
    fty[y] = fields.astype(F32).T.astype(BF)
    send(fty.at[y], fty.at[y], SEM["fy"], at_y(1))
    send(fty.at[y], fty.at[y], SEM["fy"] + 1, at_y(3))
    gram_x(0)
    for k in range(1, Y):
        arrived(eg.at[(y + 4 - k) % 4], SEM["ey"] + k)
    mean = jnp.sum(jnp.sum(eg[...].reshape(32, 128), axis=0, keepdims=True), axis=1, keepdims=True) / SAMPLES
    shifted = jnp.concatenate([eg[yy, 2 * p + zp] for zp in range(2) for yy in range(Y)], axis=1) - mean
    high = shifted.astype(BF).astype(F32)
    rest = shifted - high
    middle = rest.astype(BF).astype(F32)
    low = rest - middle
    row = lax.broadcasted_iota(jnp.int32, (16, PANEL_ROWS), 0)
    pieces = jnp.where(row == 0, high, jnp.where(row == 1, middle, jnp.where(row == 2, low, 0.0)))
    load_d.wait()
    solved = jnp.sum(
        lax.dot_general(pieces.astype(BF), dg[...], CONTRACT, preferred_element_type=F32), axis=0, keepdims=True
    )
    panel_wait(pf, SEM["pf"])
    gram_start(1, field_rows, pf[...].reshape(PANEL_ROWS, 256))
    gram_x(1)
    gram_z(0)
    for t in (0, 2, 1):
        t_arrive(t)
        t_begin(2 * t)
        t_begin(2 * t + 1)
    gram_z(1)
    for k in range(2):
        passed = fty.at[(y + (3, 1)[k]) % Y]
        arrived(passed, SEM["fy"] + k)
        part = fty.at[(y + (3, 1)[k]) % Y, pl.ds(128 * k, 128)]
        send(part, part, SEM["fy"] + 2 + k, at_y((1, 3)[k]))
    spin_total = gram_end(0)
    for u in (0, 1, 4, 5):
        t_cross(u, 0)
        t_cross(u, 1)
    field_total = gram_end(1)
    gram_column = (spin_total / SPIN_SITES * (field_total / HIDDEN_UNITS)).astype(BF)
    factor = lax.dot_general(gram_column, dg[...], CONTRACT, preferred_element_type=F32)
    factor_out[...] = factor.astype(BF)

    sample = lax.broadcasted_iota(jnp.int32, (16, PANEL_ROWS), 0)
    column = lax.broadcasted_iota(jnp.int32, (16, PANEL_ROWS), 1)
    picked = jnp.sum(
        jnp.where(column == slot * 128 + q * 16 + sample, solved, 0.0), axis=1, keepdims=True
    )
    carried = jnp.sum(factor * solved, axis=1, keepdims=True)
    narrow_row = lax.broadcasted_iota(jnp.int32, (16, 128), 0)
    narrow_col = lax.broadcasted_iota(jnp.int32, (16, 128), 1)
    here = narrow_col == q * 16 + narrow_row
    own = jnp.sum(jnp.where(here, energy_row, 0.0), axis=1, keepdims=True)
    in_panel = jnp.broadcast_to(p, (16, 1)) == j
    update = jnp.where(in_panel, picked, own - mean - carried)
    update_out[...] = jnp.sum(
        jnp.where(narrow_row == narrow_col, update, 0.0), axis=0, keepdims=True
    )
    u1[q] = jnp.sum(jnp.where(here, update, 0.0), axis=0, keepdims=True)
    for d in range(1, Q):
        send(u1.at[q], u1.at[q], SEM["uq"] + d, (wide, (q + d) % Q))
    for u in (2, 3):
        t_cross(u, 0)
        t_cross(u, 1)
    for d in range(1, Q):
        arrived(u1.at[(q + Q - d) % Q], SEM["uq"] + d)
    u2[y, j] = jnp.sum(u1[...].reshape(Q, 128), axis=0, keepdims=True)
    plane = [(kz, ky) for kz in (0, 1, 3, 2) for ky in (0, 1, 3, 2)][1:]
    for kz, ky in plane:
        device = ((2 * ((j + kz) % 4) + par) * Y + (y + ky) % Y, q)
        send(u2.at[y, j], u2.at[y, j], SEM["up"] + 4 * kz + ky, device)
    for u in range(6):
        t_cross(u, 2)
    for u in range(6):
        t_end(u)
    for k in range(2):
        arrived(fty.at[(y + 2) % Y, pl.ds(128 * k, 128)], SEM["fy"] + 2 + k)
    for kz, ky in plane:
        arrived(u2.at[(y + 4 - ky) % Y, (j + 4 - kz) % 4], SEM["up"] + 4 * kz + ky)
    for yy in range(Y):
        coefficient = jnp.concatenate([u2[yy, zi] for zi in range(4)], axis=1)
        wt[yy] = (fty[yy].astype(F32) * coefficient).astype(BF)

    mine_y = pl.ds(pl.multiple_of(y * 128, 128), 128)

    def sites(i, k):
        z1 = (z + FAR[i]) % Z
        if k == 0:
            return sp[z1, :, :, mine_y].reshape(512, 128)
        return s2[z1, (y + k) % Y].reshape(512, 128)

    for i in range(0, Z, 2):
        product = None
        for k in range(Y):
            both = jnp.concatenate([sites(i, k), sites(i + 1, k)], axis=1)
            term = jnp.dot(wt[(y + k) % Y], both, preferred_element_type=F32)
            product = term if product is None else product + term
        for n in range(2):
            value = product[:, n * 128 : (n + 1) * 128].astype(BF)
            off = FAR[i + n]
            if off == 0:
                r3[z] = value
            else:
                zb[i + n] = value
                send(zb.at[i + n], r3.at[z], SEM["r3"] + off, at_z((z + off) % Z))
    for d in range(1, Z):
        arrived(r3.at[(z + d) % Z], SEM["r3"] + Z - d)
    for copy in sends:
        copy.wait_send()


def finish(terms, factor, update, grad_out, factor_out, update_out):
    factor_out[...] = factor[...]
    update_out[...] = update[0, :16]
    for jj in range(4):
        block = terms[2 * jj].astype(F32) + terms[2 * jj + 1].astype(F32)
        grad_out[:, jj * 256 : (jj + 1) * 256] = block.T / math.sqrt(SAMPLES)


def local(spins, weights, field_bias, energies, panel_index, diag_inverse):
    vmem = pl.BlockSpec(memory_space=pltpu.VMEM)
    anywhere = pl.BlockSpec(memory_space=pl.ANY)
    smem = pl.BlockSpec(memory_space=pltpu.SMEM)
    terms, factor, update = pl.pallas_call(
        kernel,
        out_shape=(
            jax.ShapeDtypeStruct((Z, 256, 128), BF),
            jax.ShapeDtypeStruct((16, PANEL_ROWS), BF),
            jax.ShapeDtypeStruct((1, 128), F32),
        ),
        in_specs=[anywhere, anywhere, vmem, vmem, smem, anywhere],
        out_specs=(vmem, vmem, vmem),
        scratch_shapes=[
            pltpu.VMEM((Q, 128, 512), jnp.int32),
            pltpu.VMEM((Q, 4, 128, 512), BF),
            pltpu.VMEM((32, 128, 256), BF),
            pltpu.VMEM((PANEL_ROWS, PANEL_ROWS), BF),
            pltpu.VMEM((4, X, C, 16, 256), BF),
            pltpu.VMEM((Y, Z, 1, 128), F32),
            pltpu.VMEM((8, 128, 128), BF),
            pltpu.VMEM((8, 128, 256), BF),
            pltpu.VMEM((2, 256, PANEL_ROWS), BF),
            pltpu.VMEM((2, 256, PANEL_ROWS), F32),
            pltpu.VMEM((2, 256, PANEL_ROWS), BF),
            pltpu.VMEM((2, 4, 64, PANEL_ROWS), BF),
            pltpu.VMEM((2, 4, 64, PANEL_ROWS), BF),
            pltpu.VMEM((2, 4, 16, PANEL_ROWS), F32),
            pltpu.VMEM((2, 4, 16, PANEL_ROWS), BF),
            pltpu.VMEM((2, 4, 16, PANEL_ROWS), BF),
            pltpu.VMEM((Q, 1, 128), F32),
            pltpu.VMEM((Y, 4, 1, 128), F32),
            pltpu.VMEM((Y, 256, 512), BF),
            pltpu.VMEM((Q, Y, 4, 128, 128), BF),
            pltpu.VMEM((Y, 256, 512), BF),
            pltpu.VMEM((Z, 256, 128), BF),
            pltpu.SemaphoreType.DMA((NSEM,)),
            pltpu.SemaphoreType.DMA((NSEM,)),
            pltpu.SemaphoreType.DMA((10,)),
        ],
        compiler_params=pltpu.CompilerParams(
            collective_id=0, has_side_effects=True, vmem_limit_bytes=56 * 1024 * 1024
        ),
    )(
        spins,
        weights,
        field_bias.reshape(1, -1),
        energies,
        panel_index,
        diag_inverse,
    )
    return pl.pallas_call(
        finish,
        out_shape=(
            jax.ShapeDtypeStruct((128, 1024), F32),
            jax.ShapeDtypeStruct((16, PANEL_ROWS), BF),
            jax.ShapeDtypeStruct((16,), F32),
        ),
        in_specs=[vmem, vmem, vmem],
        out_specs=(vmem, vmem, vmem),
    )(terms, factor, update)


def solution(mesh):
    in_specs = (P("wide", None), P("wide", "narrow"), P("narrow"), P("wide"), P(), P())
    out_specs = (P("wide", "narrow"), P(("wide", "narrow"), None), P(("wide", "narrow")))
    return jax.shard_map(local, mesh=mesh, in_specs=in_specs, out_specs=out_specs, check_vma=False)
```

```python
import functools
import math

import jax
import jax.numpy as jnp
from jax import lax
from jax.experimental import pallas as pl
from jax.experimental.pallas import tpu as pltpu
from jax.sharding import PartitionSpec as P

SPIN_SITES = 4096
HIDDEN_UNITS = 8192
PANEL_ROWS = 1024
SAMPLES = 4096
Z, Y, X, C = 8, 4, 4, 2
Q = X * C
NEAR = (0, 1, -1, -2, 2, -3, 3, 4)
SAME = (2, 6, 4)
GRAMS = ((0, 0, 1024), (1, 0, 512), (1, 512, 512))
UNITS = ((0, 0), (1, 1), (0, 1), (1, 0), (2, 0), (2, 1))
MESH = pl.DeviceIdType.MESH
BF = jnp.bfloat16
F32 = jnp.float32
CONTRACT = (((1,), (1,)), ((), ()))


class Sems:
    def __init__(self):
        self.n = 0

    def take(self, n):
        self.n += n
        return self.n - n


def layout():
    s = Sems()
    names = dict(
        wz=8, wy=24, sz=6, sx=18, sc=24, ty=4, tx=18, tc=24, ez=8, ey=4, ps=7, pf=7, fy=4,
        gc=3, gx=12, gz=12, uq=8, up=16, r3=8, rel=2,
    )
    return {k: s.take(n) for k, n in names.items()}, s.n


SEM, NSEM = layout()


def kernel(
    spins, weights, bias, energy, panel, diag,
    r3, factor_out, update_out,
    s32, sp, wg, dg, f5, eg, psp, pf,
    ftot, gsend, gkeep, grecv, xsend, xrecv, tsum, zsend, zrecv,
    u1, u2, wt, s2, fty, zb, rel, nearsum,
    ssem, rsem, lsem,
):
    wide = lax.axis_index("wide")
    q = lax.axis_index("narrow")
    z, y = wide // Y, wide % Y
    x, c = q // C, q % C
    par, j = z % 2, z // 2
    sib = x * C + (1 - c)
    sign = 1 - 2 * par
    partner = z + sign
    sends = []

    def at_z(zz):
        return (zz * Y + y, q)

    def at_y(k):
        return (z * Y + (y + k) % Y, q)

    def at_x(k):
        return (wide, ((x + k) % X) * C + c)

    def send(src, dst, index, device):
        copy = pltpu.make_async_remote_copy(
            src_ref=src, dst_ref=dst, send_sem=ssem.at[index], recv_sem=rsem.at[index],
            device_id=device, device_id_type=MESH,
        )
        copy.start()
        sends.append(copy)

    def arrived(dst, index):
        pltpu.make_async_remote_copy(
            src_ref=dst, dst_ref=dst, send_sem=ssem.at[index], recv_sem=rsem.at[index],
            device_id=(wide, sib), device_id_type=MESH,
        ).wait_recv()

    def load_spins(k):
        return pltpu.make_async_copy(spins.at[:, pl.ds(pl.multiple_of(k * 512, 512), 512)], s32.at[k], lsem.at[k])

    for d in range(Q):
        load_spins((q + d) % Q).start()
    my_w = weights.at[:, pl.ds(pl.multiple_of(j * 256, 256), 256)]
    load_w = pltpu.make_async_copy(my_w, wg.at[wide], lsem.at[8])
    load_w.start()
    load_d = pltpu.make_async_copy(diag, dg, lsem.at[9])
    load_d.start()

    barrier = pltpu.get_barrier_semaphore()
    for d in range(1, Z):
        pl.semaphore_signal(barrier, inc=1, device_id=at_z((z + d) % Z), device_id_type=MESH)
    for k in range(1, Y):
        pl.semaphore_signal(barrier, inc=1, device_id=at_y(k), device_id_type=MESH)
    for d in range(1, Q):
        pl.semaphore_signal(barrier, inc=1, device_id=(wide, (q + d) % Q), device_id_type=MESH)

    def convert(k):
        load_spins(k).wait()
        sp[k, j] = s32[k].astype(F32).astype(BF)

    convert(q)
    energy_row = energy[...].astype(F32).reshape(1, 128)
    eg[y, z] = energy_row
    load_w.wait()
    pl.semaphore_wait(barrier, Z + Y + Q - 3)

    def w_y(i, z1):
        chunk = wg.at[z1 * Y + y]
        send(chunk, chunk, SEM["wy"] + i, at_y(1))
        send(chunk, chunk, SEM["wy"] + 8 + i, at_y(-1 + Y))

    def toward(o):
        return (z + sign * o + Z) % Z

    def w_z(o):
        zd = toward(o)
        src = weights.at[:, pl.ds(pl.multiple_of((zd // 2) * 256, 256), 256)]
        seen = {1: 1, -1: -1, 2: -2, -3: -3}[o]
        send(src, wg.at[wide], SEM["wz"] + 3 + seen, at_z(zd))

    def s_z(u):
        t, h = UNITS[u]
        mine = sp.at[q, j, pl.ds(64 * h, 64)]
        send(mine, mine, SEM["sz"] + u, at_z((z + (6, 2)[t]) % Z))

    w_y(0, z)
    s_z(0)
    s_z(1)
    w_z(1)
    w_z(-1)
    s_z(2)
    s_z(3)
    w_z(2)
    w_z(-3)
    for d in range(1, Z):
        send(eg.at[y, z], eg.at[y, z], SEM["ez"] + d, at_z((z + d) % Z))
    for d in range(1, Q):
        convert((q + d) % Q)
    for o in (3, 4):
        r3[toward(o)] = jnp.zeros((256, 128), BF)

    def w_take(i):
        o = NEAR[i]
        z1 = toward(o)
        chunk = wg.at[z1 * Y + y]
        arrived(chunk, SEM["wz"] + 3 + o)
        if o < 0:
            send(chunk, chunk, SEM["wz"] + 4 - o, at_z(partner))
        w_y(i, z1)

    def w_relay(i):
        z1 = toward(NEAR[i])
        if i % 2 == 0:
            chunk = wg.at[z1 * Y + (y + 3) % Y]
            arrived(chunk, SEM["wy"] + i)
            send(chunk, chunk, SEM["wy"] + 16 + i, at_y(1))
        else:
            chunk = wg.at[z1 * Y + (y + 1) % Y]
            arrived(chunk, SEM["wy"] + 8 + i)
            send(chunk, chunk, SEM["wy"] + 16 + i, at_y(3))

    def zi_of(t):
        return ((z + SAME[t]) % Z) // 2

    def s_piece(source, u):
        t, h = UNITS[u]
        return sp.at[source, zi_of(t), pl.ds(64 * h, 64)]

    def s_arrive(u):
        got = s_piece(q, u)
        arrived(got, SEM["sz"] + u)
        if u < 2:
            send(got, got, SEM["sz"] + 4 + u, at_z((z + (6, 2)[u]) % Z))

    def spread(piece, bx, bc):
        def begin(u):
            mine = piece(q, u)
            send(mine, mine, bx + u, at_x(1))
            send(mine, mine, bx + 6 + u, at_x(3))
            send(mine, mine, bc + u, (wide, sib))

        def cross(u, k):
            source = ((x + (3, 1, 2)[k]) % X) * C + c
            got = piece(source, u)
            arrived(got, bx + 6 * k + u)
            if k == u % 2:
                send(got, got, bx + 12 + u, at_x((1, 3)[k]))
            send(got, got, bc + 6 * (k + 1) + u, (wide, sib))

        def end(u):
            for k in range(4):
                source = ((x + (0, 3, 1, 2)[k]) % X) * C + (1 - c)
                arrived(piece(source, u), bc + 6 * k + u)

        return begin, cross, end

    s_begin, s_cross, s_end = spread(s_piece, SEM["sx"], SEM["sc"])
    t_begin, t_cross, t_end = spread(
        lambda source, u: s2.at[source, (y + u // 2 + 1) % Y, pl.ds(2 * (u % 2), 2)], SEM["tx"], SEM["tc"]
    )

    def t_send(k):
        columns = pl.ds(pl.multiple_of(((y + k) % Y) * 128, 128), 128)
        send(sp.at[q, :, :, columns], s2.at[q, y], SEM["ty"] + k, at_y(k))

    def t_arrive(t):
        arrived(s2.at[q, (y + t + 1) % Y], SEM["ty"] + Y - 1 - t)

    p = panel[0]
    slot = par * 4 + y
    other = (1 - par) * 4 + y

    def panel_send(buf, base):
        send(buf.at[slot], buf.at[slot], base, at_z(partner))
        for k in (1, 3, 2):
            send(buf.at[slot], buf.at[slot], base + k, at_y(k))

    def panel_pass(buf, base):
        arrived(buf.at[other], base)
        for k in (1, 3, 2):
            send(buf.at[other], buf.at[other], base + 3 + k, at_y(k))

    def panel_wait(buf, base, half):
        for k in (1, 3, 2):
            group = (1 - par) if half else par
            arrived(buf.at[group * 4 + (y + 4 - k) % 4], base + 3 * half + k)

    sub = pl.ds(pl.multiple_of(j * 128, 128), 128)

    def gram_start(part, rows_of, rhs):
        g, first, width = GRAMS[part]
        columns = pl.ds(first, width)
        theirs = lax.dot_general(rows_of(1 - c), rhs, CONTRACT, preferred_element_type=F32)
        gsend[g, :, columns] = theirs.astype(BF)
        send(gsend.at[g, :, columns], grecv.at[g, :, columns], SEM["gc"] + part, (wide, sib))
        gkeep[g, :, columns] = lax.dot_general(rows_of(c), rhs, CONTRACT, preferred_element_type=F32)

    def spin_rows(cc):
        return jnp.concatenate(
            [
                sp[q, zi, pl.ds(pl.multiple_of((2 * xx + cc) * 16, 16), 16), sub]
                for xx in range(X)
                for zi in range(4)
            ],
            axis=0,
        )

    def gram_x(part):
        g, first, width = GRAMS[part]
        columns = pl.ds(first, width)
        arrived(grecv.at[g, :, columns], SEM["gc"] + part)
        for k in (2, 1, 3):
            rows = pl.ds(pl.multiple_of(((x + k) % X) * 64, 64), 64)
            value = gkeep[g, rows, columns] + grecv[g, rows, columns].astype(F32)
            xsend[g, k, :, columns] = value.astype(BF)
            send(xsend.at[g, k, :, columns], xrecv.at[g, k, :, columns], SEM["gx"] + 4 * part + k, at_x(k))

    def gram_z(part):
        g, first, width = GRAMS[part]
        columns = pl.ds(first, width)
        rows = pl.ds(pl.multiple_of(x * 64, 64), 64)
        value = gkeep[g, rows, columns] + grecv[g, rows, columns].astype(F32)
        for k in (1, 3, 2):
            arrived(xrecv.at[g, k, :, columns], SEM["gx"] + 4 * part + k)
            value = value + xrecv[g, k, :, columns].astype(F32)
        tsum[g, :, :, columns] = value.reshape(4, 16, width)
        for k in (2, 1, 3):
            zi = (j + k) % 4
            zsend[g, k, :, columns] = tsum[g, zi, :, columns].astype(BF)
            send(
                zsend.at[g, k, :, columns],
                zrecv.at[g, k, :, columns],
                SEM["gz"] + 4 * part + k,
                at_z(2 * zi + par),
            )

    def gram_end(part):
        g, first, width = GRAMS[part]
        columns = pl.ds(first, width)
        value = tsum[g, j, :, columns]
        for k in (1, 3, 2):
            arrived(zrecv.at[g, k, :, columns], SEM["gz"] + 4 * part + k)
            value = value + zrecv[g, k, :, columns].astype(F32)
        return value

    def field_rows(cc):
        return jnp.concatenate([f5[zi, xx, cc] for xx in range(X) for zi in range(4)], axis=0)

    s_arrive(0)
    s_begin(0)
    s_arrive(1)
    s_begin(1)
    w_take(1)
    w_take(2)
    s_arrive(2)
    s_begin(2)
    s_arrive(3)
    s_begin(3)
    w_relay(0)
    s_cross(0, 0)
    s_cross(0, 1)
    s_cross(1, 0)
    s_cross(1, 1)
    w_take(3)
    w_relay(1)
    s_arrive(4)
    s_begin(4)
    s_arrive(5)
    s_begin(5)
    w_relay(2)
    chosen = sp[q, 0, :, sub].astype(F32)
    for zi in range(1, 4):
        chosen = jnp.where(p == zi, sp[q, zi, :, sub].astype(F32), chosen)
    psp[slot] = chosen.astype(BF)
    panel_send(psp, SEM["ps"])
    s_cross(2, 0)
    s_cross(2, 1)
    s_cross(3, 0)
    s_cross(3, 1)
    w_take(4)
    w_relay(3)
    w_take(5)
    w_take(6)
    w_relay(4)
    s_cross(0, 2)
    s_cross(1, 2)
    s_cross(2, 2)
    s_cross(3, 2)
    panel_pass(psp, SEM["ps"])
    s_cross(4, 0)
    s_cross(4, 1)
    s_cross(5, 0)
    s_cross(5, 1)
    w_take(7)
    w_relay(5)
    for d in range(1, Z):
        arrived(eg.at[y, (z + d) % Z], SEM["ez"] + Z - d)
    for k in range(1, Y):
        send(eg.at[y], eg.at[y], SEM["ey"] + k, at_y(k))
    w_relay(6)
    panel_wait(psp, SEM["ps"], 0)
    panel_wait(psp, SEM["ps"], 1)
    gram_start(0, spin_rows, psp[...].reshape(PANEL_ROWS, 128))
    w_relay(7)
    s_cross(4, 2)
    s_cross(5, 2)
    gram_x(0)

    for u in range(6):
        s_end(u)
    total = None
    for i in range(Z):
        z1 = toward(NEAR[i])
        if i % 2 == 0:
            arrived(wg.at[z1 * Y + (y + 1) % Y], SEM["wy"] + 8 + i)
        else:
            arrived(wg.at[z1 * Y + (y + 3) % Y], SEM["wy"] + i)
        arrived(wg.at[z1 * Y + (y + 2) % Y], SEM["wy"] + 16 + i)
        term = jnp.dot(
            sp[z1].reshape(512, 512), wg[pl.ds(z1 * Y, Y)].reshape(512, 256), preferred_element_type=F32
        )
        total = term if total is None else total + term
    mine = bias[:, pl.ds(pl.multiple_of(j * 256, 256), 256)]
    fields = jnp.tanh(total + mine).astype(BF)
    f5[...] = fields.reshape(4, X, C, 16, 256)
    pf[slot] = f5[p].reshape(128, 256)
    panel_send(pf, SEM["pf"])

    fty[y] = fields.astype(F32).T.astype(BF)
    panel_pass(pf, SEM["pf"])
    for k in (1, 3, 2):
        t_send(k)
    send(fty.at[y], fty.at[y], SEM["fy"], at_y(1))
    send(fty.at[y], fty.at[y], SEM["fy"] + 1, at_y(3))
    panel_wait(pf, SEM["pf"], 0)
    gram_start(1, field_rows, pf[pl.ds(par * 4, 4)].reshape(512, 256))
    gram_x(1)
    for k in range(1, Y):
        arrived(eg.at[(y + 4 - k) % 4], SEM["ey"] + k)
    mean = jnp.sum(jnp.sum(eg[...].reshape(32, 128), axis=0, keepdims=True), axis=1, keepdims=True) / SAMPLES
    shifted = jnp.concatenate([eg[yy, 2 * p + zp] for zp in range(2) for yy in range(Y)], axis=1) - mean
    high = shifted.astype(BF).astype(F32)
    rest = shifted - high
    middle = rest.astype(BF).astype(F32)
    low = rest - middle
    row = lax.broadcasted_iota(jnp.int32, (16, PANEL_ROWS), 0)
    pieces = jnp.where(row == 0, high, jnp.where(row == 1, middle, jnp.where(row == 2, low, 0.0)))
    load_d.wait()
    solved = jnp.sum(
        lax.dot_general(pieces.astype(BF), dg[...], CONTRACT, preferred_element_type=F32), axis=0, keepdims=True
    )
    panel_wait(pf, SEM["pf"], 1)
    gram_start(2, field_rows, pf[pl.ds((1 - par) * 4, 4)].reshape(512, 256))
    gram_x(2)
    t_arrive(0)
    t_begin(0)
    t_begin(1)
    t_arrive(2)
    t_begin(4)
    t_begin(5)
    gram_z(0)
    gram_z(1)
    t_arrive(1)
    t_begin(2)
    t_begin(3)
    gram_z(2)
    for k in range(2):
        passed = fty.at[(y + (3, 1)[k]) % Y]
        arrived(passed, SEM["fy"] + k)
        part = fty.at[(y + (3, 1)[k]) % Y, pl.ds(128 * k, 128)]
        send(part, part, SEM["fy"] + 2 + k, at_y((1, 3)[k]))
    t_cross(0, 0)
    t_cross(0, 1)
    t_cross(1, 0)
    t_cross(1, 1)
    spin_total = gram_end(0)
    ftot[:, pl.ds(pl.multiple_of(par * 512, 512), 512)] = gram_end(1)
    ftot[:, pl.ds(pl.multiple_of((1 - par) * 512, 512), 512)] = gram_end(2)
    field_total = ftot[...]
    gram_column = (spin_total / SPIN_SITES * (field_total / HIDDEN_UNITS)).astype(BF)
    factor = lax.dot_general(gram_column, dg[...], CONTRACT, preferred_element_type=F32)
    factor_out[...] = factor.astype(BF)

    sample = lax.broadcasted_iota(jnp.int32, (16, PANEL_ROWS), 0)
    column = lax.broadcasted_iota(jnp.int32, (16, PANEL_ROWS), 1)
    picked = jnp.sum(
        jnp.where(column == slot * 128 + q * 16 + sample, solved, 0.0), axis=1, keepdims=True
    )
    carried = jnp.sum(factor * solved, axis=1, keepdims=True)
    narrow_row = lax.broadcasted_iota(jnp.int32, (16, 128), 0)
    narrow_col = lax.broadcasted_iota(jnp.int32, (16, 128), 1)
    here = narrow_col == q * 16 + narrow_row
    own = jnp.sum(jnp.where(here, energy_row, 0.0), axis=1, keepdims=True)
    in_panel = jnp.broadcast_to(p, (16, 1)) == j
    update = jnp.where(in_panel, picked, own - mean - carried)
    update_out[...] = jnp.sum(
        jnp.where(narrow_row == narrow_col, update, 0.0), axis=0, keepdims=True
    )
    u1[q] = jnp.sum(jnp.where(here, update, 0.0), axis=0, keepdims=True)
    for d in range(1, Q):
        send(u1.at[q], u1.at[q], SEM["uq"] + d, (wide, (q + d) % Q))
    t_cross(4, 0)
    t_cross(4, 1)
    t_cross(5, 0)
    t_cross(5, 1)
    t_cross(2, 0)
    t_cross(2, 1)
    t_cross(3, 0)
    t_cross(3, 1)
    for d in range(1, Q):
        arrived(u1.at[(q + Q - d) % Q], SEM["uq"] + d)
    u2[y, j] = jnp.sum(u1[...].reshape(Q, 128), axis=0, keepdims=True)
    plane = [(kz, ky) for kz in (0, 1, 3, 2) for ky in (0, 1, 3, 2)][1:]
    for kz, ky in plane:
        device = ((2 * ((j + kz) % 4) + par) * Y + (y + ky) % Y, q)
        send(u2.at[y, j], u2.at[y, j], SEM["up"] + 4 * kz + ky, device)
    for u in range(6):
        t_cross(u, 2)
    for u in range(6):
        t_end(u)
    for k in range(2):
        arrived(fty.at[(y + 2) % Y, pl.ds(128 * k, 128)], SEM["fy"] + 2 + k)
    for kz, ky in plane:
        arrived(u2.at[(y + 4 - ky) % Y, (j + 4 - kz) % 4], SEM["up"] + 4 * kz + ky)
    for yy in range(Y):
        coefficient = jnp.concatenate([u2[yy, zi] for zi in range(4)], axis=1)
        wt[yy] = (fty[yy].astype(F32) * coefficient).astype(BF)

    mine_y = pl.ds(pl.multiple_of(y * 128, 128), 128)

    def sites(o, k):
        if k == 0:
            return sp[toward(o), :, :, mine_y].reshape(512, 128)
        return s2[toward(o), (y + k) % Y].reshape(512, 128)

    def products(first, second):
        product = None
        for k in range(Y):
            both = jnp.concatenate([sites(first, k), sites(second, k)], axis=1)
            term = jnp.dot(wt[(y + k) % Y], both, preferred_element_type=F32)
            product = term if product is None else product + term
        return product[:, :128], product[:, 128:]

    def to_owner(o, value):
        seen = {1: 1, 2: -2, -1: -1, -3: -3, -2: 2}[o]
        zb[o + 3] = value.astype(BF)
        send(zb.at[o + 3], r3.at[z], SEM["r3"] + 3 + seen, at_z(toward(o)))

    for n in range(2):
        away, near = products(4 - n, n - 3)
        zb[7 - n] = away.astype(BF)
        send(zb.at[7 - n], rel.at[n], SEM["rel"] + n, at_z(partner))
        nearsum[n] = near

    def relay_sum(n):
        arrived(rel.at[n], SEM["rel"] + n)
        to_owner(n - 3, nearsum[n] + rel[n].astype(F32))

    ahead, behind = products(2, -1)
    to_owner(2, ahead)
    relay_sum(0)
    to_owner(-1, behind)
    ahead, own_term = products(1, 0)
    r3[z] = own_term.astype(BF)
    relay_sum(1)
    to_owner(1, ahead)
    for o in (-3, 2, -2, -1, 1):
        arrived(r3.at[toward(o)], SEM["r3"] + 3 + o)
    for copy in sends:
        copy.wait_send()


def finish(terms, factor, update, grad_out, factor_out, update_out):
    factor_out[...] = factor[...]
    update_out[...] = update[0, :16]
    for jj in range(4):
        block = terms[2 * jj].astype(F32) + terms[2 * jj + 1].astype(F32)
        grad_out[:, jj * 256 : (jj + 1) * 256] = block.T / math.sqrt(SAMPLES)


def local(spins, weights, field_bias, energies, panel_index, diag_inverse):
    vmem = pl.BlockSpec(memory_space=pltpu.VMEM)
    anywhere = pl.BlockSpec(memory_space=pl.ANY)
    smem = pl.BlockSpec(memory_space=pltpu.SMEM)
    terms, factor, update = pl.pallas_call(
        kernel,
        out_shape=(
            jax.ShapeDtypeStruct((Z, 256, 128), BF),
            jax.ShapeDtypeStruct((16, PANEL_ROWS), BF),
            jax.ShapeDtypeStruct((1, 128), F32),
        ),
        in_specs=[anywhere, anywhere, vmem, vmem, smem, anywhere],
        out_specs=(vmem, vmem, vmem),
        scratch_shapes=[
            pltpu.VMEM((Q, 128, 512), jnp.int32),
            pltpu.VMEM((Q, 4, 128, 512), BF),
            pltpu.VMEM((32, 128, 256), BF),
            pltpu.VMEM((PANEL_ROWS, PANEL_ROWS), BF),
            pltpu.VMEM((4, X, C, 16, 256), BF),
            pltpu.VMEM((Y, Z, 1, 128), F32),
            pltpu.VMEM((8, 128, 128), BF),
            pltpu.VMEM((8, 128, 256), BF),
            pltpu.VMEM((16, PANEL_ROWS), F32),
            pltpu.VMEM((2, 256, PANEL_ROWS), BF),
            pltpu.VMEM((2, 256, PANEL_ROWS), F32),
            pltpu.VMEM((2, 256, PANEL_ROWS), BF),
            pltpu.VMEM((2, 4, 64, PANEL_ROWS), BF),
            pltpu.VMEM((2, 4, 64, PANEL_ROWS), BF),
            pltpu.VMEM((2, 4, 16, PANEL_ROWS), F32),
            pltpu.VMEM((2, 4, 16, PANEL_ROWS), BF),
            pltpu.VMEM((2, 4, 16, PANEL_ROWS), BF),
            pltpu.VMEM((Q, 1, 128), F32),
            pltpu.VMEM((Y, 4, 1, 128), F32),
            pltpu.VMEM((Y, 256, 512), BF),
            pltpu.VMEM((Q, Y, 4, 128, 128), BF),
            pltpu.VMEM((Y, 256, 512), BF),
            pltpu.VMEM((Z, 256, 128), BF),
            pltpu.VMEM((2, 256, 128), BF),
            pltpu.VMEM((2, 256, 128), F32),
            pltpu.SemaphoreType.DMA((NSEM,)),
            pltpu.SemaphoreType.DMA((NSEM,)),
            pltpu.SemaphoreType.DMA((10,)),
        ],
        compiler_params=pltpu.CompilerParams(
            collective_id=0, has_side_effects=True, vmem_limit_bytes=56 * 1024 * 1024
        ),
    )(
        spins,
        weights,
        field_bias.reshape(1, -1),
        energies,
        panel_index,
        diag_inverse,
    )
    return pl.pallas_call(
        finish,
        out_shape=(
            jax.ShapeDtypeStruct((128, 1024), F32),
            jax.ShapeDtypeStruct((16, PANEL_ROWS), BF),
            jax.ShapeDtypeStruct((16,), F32),
        ),
        in_specs=[vmem, vmem, vmem],
        out_specs=(vmem, vmem, vmem),
    )(terms, factor, update)


def solution(mesh):
    in_specs = (P("wide", None), P("wide", "narrow"), P("narrow"), P("wide"), P(), P())
    out_specs = (P("wide", "narrow"), P(("wide", "narrow"), None), P(("wide", "narrow")))
    return jax.shard_map(local, mesh=mesh, in_specs=in_specs, out_specs=out_specs, check_vma=False)
```

```python
import functools
import math

import jax
import jax.numpy as jnp
from jax import lax
from jax.experimental import pallas as pl
from jax.experimental.pallas import tpu as pltpu
from jax.sharding import PartitionSpec as P

SPIN_SITES = 4096
HIDDEN_UNITS = 8192
PANEL_ROWS = 1024
SAMPLES = 4096
Z, Y, X, C = 8, 4, 4, 2
Q = X * C
NEAR = (0, 1, -1, -2, 2, -3, 3, 4)
SAME = (2, 6, 4)
GRAMS = ((0, 0, 1024), (1, 0, 512), (1, 512, 512))
UNITS = ((0, 0), (1, 1), (0, 1), (1, 0), (2, 0), (2, 1))
MESH = pl.DeviceIdType.MESH
BF = jnp.bfloat16
F32 = jnp.float32
CONTRACT = (((1,), (1,)), ((), ()))


class Sems:
    def __init__(self):
        self.n = 0

    def take(self, n):
        self.n += n
        return self.n - n


def layout():
    s = Sems()
    names = dict(
        wz=8, wy=24, sz=6, sx=18, sc=24, ty=4, tx=18, tc=24, ez=8, ey=4, ps=7, pf=7, fy=4,
        gc=3, gx=12, gz=12, uq=8, up=16, r3=8, rel=2,
    )
    return {k: s.take(n) for k, n in names.items()}, s.n


SEM, NSEM = layout()


def kernel(
    spins, weights, bias, energy, panel, diag,
    r3, factor_out, update_out,
    s32, sp, wg, dg, f5, eg, psp, pf,
    ftot, gsend, gkeep, grecv, xsend, xrecv, tsum, zsend, zrecv,
    u1, u2, wt, s2, fty, zb, rel, nearsum,
    ssem, rsem, lsem,
):
    wide = lax.axis_index("wide")
    q = lax.axis_index("narrow")
    z, y = wide // Y, wide % Y
    x, c = q // C, q % C
    par, j = z % 2, z // 2
    sib = x * C + (1 - c)
    sign = 1 - 2 * par
    partner = z + sign
    sends = []

    def at_z(zz):
        return (zz * Y + y, q)

    def at_y(k):
        return (z * Y + (y + k) % Y, q)

    def at_x(k):
        return (wide, ((x + k) % X) * C + c)

    def send(src, dst, index, device):
        copy = pltpu.make_async_remote_copy(
            src_ref=src, dst_ref=dst, send_sem=ssem.at[index], recv_sem=rsem.at[index],
            device_id=device, device_id_type=MESH,
        )
        copy.start()
        sends.append(copy)

    def arrived(dst, index):
        pltpu.make_async_remote_copy(
            src_ref=dst, dst_ref=dst, send_sem=ssem.at[index], recv_sem=rsem.at[index],
            device_id=(wide, sib), device_id_type=MESH,
        ).wait_recv()

    def load_spins(k):
        return pltpu.make_async_copy(spins.at[:, pl.ds(pl.multiple_of(k * 512, 512), 512)], s32.at[k], lsem.at[k])

    for d in range(Q):
        load_spins((q + d) % Q).start()
    my_w = weights.at[:, pl.ds(pl.multiple_of(j * 256, 256), 256)]
    load_w = pltpu.make_async_copy(my_w, wg.at[wide], lsem.at[8])
    load_w.start()
    load_d = pltpu.make_async_copy(diag, dg, lsem.at[9])
    load_d.start()

    barrier = pltpu.get_barrier_semaphore()
    for d in range(1, Z):
        pl.semaphore_signal(barrier, inc=1, device_id=at_z((z + d) % Z), device_id_type=MESH)
    for k in range(1, Y):
        pl.semaphore_signal(barrier, inc=1, device_id=at_y(k), device_id_type=MESH)
    for d in range(1, Q):
        pl.semaphore_signal(barrier, inc=1, device_id=(wide, (q + d) % Q), device_id_type=MESH)

    def convert(k):
        load_spins(k).wait()
        sp[k, j] = s32[k].astype(F32).astype(BF)

    convert(q)
    energy_row = energy[...].astype(F32).reshape(1, 128)
    eg[y, z] = energy_row
    load_w.wait()
    pl.semaphore_wait(barrier, Z + Y + Q - 3)

    def w_y(i, z1):
        chunk = wg.at[z1 * Y + y]
        send(chunk, chunk, SEM["wy"] + i, at_y(1))
        send(chunk, chunk, SEM["wy"] + 8 + i, at_y(-1 + Y))

    def toward(o):
        return (z + sign * o + Z) % Z

    def w_z(o):
        zd = toward(o)
        src = weights.at[:, pl.ds(pl.multiple_of((zd // 2) * 256, 256), 256)]
        seen = {1: 1, -1: -1, 2: -2, -3: -3}[o]
        send(src, wg.at[wide], SEM["wz"] + 3 + seen, at_z(zd))

    def s_z(u):
        t, h = UNITS[u]
        mine = sp.at[q, j, pl.ds(64 * h, 64)]
        send(mine, mine, SEM["sz"] + u, at_z((z + (6, 2)[t]) % Z))

    w_y(0, z)
    s_z(0)
    s_z(1)
    w_z(1)
    w_z(-1)
    s_z(2)
    s_z(3)
    w_z(2)
    w_z(-3)
    for d in range(1, Z):
        send(eg.at[y, z], eg.at[y, z], SEM["ez"] + d, at_z((z + d) % Z))
    for d in range(1, Q):
        convert((q + d) % Q)
    for o in (3, 4):
        r3[toward(o)] = jnp.zeros((256, 128), BF)

    def w_take(i):
        o = NEAR[i]
        z1 = toward(o)
        chunk = wg.at[z1 * Y + y]
        arrived(chunk, SEM["wz"] + 3 + o)
        if o < 0:
            send(chunk, chunk, SEM["wz"] + 4 - o, at_z(partner))
        w_y(i, z1)

    def w_relay(i):
        z1 = toward(NEAR[i])
        if i % 2 == 0:
            chunk = wg.at[z1 * Y + (y + 3) % Y]
            arrived(chunk, SEM["wy"] + i)
            send(chunk, chunk, SEM["wy"] + 16 + i, at_y(1))
        else:
            chunk = wg.at[z1 * Y + (y + 1) % Y]
            arrived(chunk, SEM["wy"] + 8 + i)
            send(chunk, chunk, SEM["wy"] + 16 + i, at_y(3))

    def zi_of(t):
        return ((z + SAME[t]) % Z) // 2

    def s_piece(source, u):
        t, h = UNITS[u]
        return sp.at[source, zi_of(t), pl.ds(64 * h, 64)]

    def s_arrive(u):
        got = s_piece(q, u)
        arrived(got, SEM["sz"] + u)
        if u < 2:
            send(got, got, SEM["sz"] + 4 + u, at_z((z + (6, 2)[u]) % Z))

    def spread(piece, bx, bc):
        def begin(u):
            mine = piece(q, u)
            send(mine, mine, bx + u, at_x(1))
            send(mine, mine, bx + 6 + u, at_x(3))
            send(mine, mine, bc + u, (wide, sib))

        def cross(u, k):
            source = ((x + (3, 1, 2)[k]) % X) * C + c
            got = piece(source, u)
            arrived(got, bx + 6 * k + u)
            if k == u % 2:
                send(got, got, bx + 12 + u, at_x((1, 3)[k]))
            send(got, got, bc + 6 * (k + 1) + u, (wide, sib))

        def end(u):
            for k in range(4):
                source = ((x + (0, 3, 1, 2)[k]) % X) * C + (1 - c)
                arrived(piece(source, u), bc + 6 * k + u)

        return begin, cross, end

    s_begin, s_cross, s_end = spread(s_piece, SEM["sx"], SEM["sc"])
    t_begin, t_cross, t_end = spread(
        lambda source, u: s2.at[source, (y + u // 2 + 1) % Y, pl.ds(2 * (u % 2), 2)], SEM["tx"], SEM["tc"]
    )

    def t_send(k):
        columns = pl.ds(pl.multiple_of(((y + k) % Y) * 128, 128), 128)
        send(sp.at[q, :, :, columns], s2.at[q, y], SEM["ty"] + k, at_y(k))

    def t_arrive(t):
        arrived(s2.at[q, (y + t + 1) % Y], SEM["ty"] + Y - 1 - t)

    p = panel[0]
    slot = par * 4 + y
    other = (1 - par) * 4 + y

    def panel_send(buf, base):
        send(buf.at[slot], buf.at[slot], base, at_z(partner))
        for k in (1, 3, 2):
            send(buf.at[slot], buf.at[slot], base + k, at_y(k))

    def panel_pass(buf, base):
        arrived(buf.at[other], base)
        for k in (1, 3, 2):
            send(buf.at[other], buf.at[other], base + 3 + k, at_y(k))

    def panel_wait(buf, base, half):
        for k in (1, 3, 2):
            group = (1 - par) if half else par
            arrived(buf.at[group * 4 + (y + 4 - k) % 4], base + 3 * half + k)

    sub = pl.ds(pl.multiple_of(j * 128, 128), 128)

    def gram_start(part, rows_of, rhs):
        g, first, width = GRAMS[part]
        columns = pl.ds(first, width)
        theirs = lax.dot_general(rows_of(1 - c), rhs, CONTRACT, preferred_element_type=F32)
        gsend[g, :, columns] = theirs.astype(BF)
        send(gsend.at[g, :, columns], grecv.at[g, :, columns], SEM["gc"] + part, (wide, sib))
        gkeep[g, :, columns] = lax.dot_general(rows_of(c), rhs, CONTRACT, preferred_element_type=F32)

    def spin_rows(cc):
        return jnp.concatenate(
            [
                sp[q, zi, pl.ds(pl.multiple_of((2 * xx + cc) * 16, 16), 16), sub]
                for xx in range(X)
                for zi in range(4)
            ],
            axis=0,
        )

    def gram_x(part):
        g, first, width = GRAMS[part]
        columns = pl.ds(first, width)
        arrived(grecv.at[g, :, columns], SEM["gc"] + part)
        for k in (2, 1, 3):
            rows = pl.ds(pl.multiple_of(((x + k) % X) * 64, 64), 64)
            value = gkeep[g, rows, columns] + grecv[g, rows, columns].astype(F32)
            xsend[g, k, :, columns] = value.astype(BF)
            send(xsend.at[g, k, :, columns], xrecv.at[g, k, :, columns], SEM["gx"] + 4 * part + k, at_x(k))

    def gram_z(part):
        g, first, width = GRAMS[part]
        columns = pl.ds(first, width)
        rows = pl.ds(pl.multiple_of(x * 64, 64), 64)
        value = gkeep[g, rows, columns] + grecv[g, rows, columns].astype(F32)
        for k in (1, 3, 2):
            arrived(xrecv.at[g, k, :, columns], SEM["gx"] + 4 * part + k)
            value = value + xrecv[g, k, :, columns].astype(F32)
        tsum[g, :, :, columns] = value.reshape(4, 16, width)
        for k in (2, 1, 3):
            zi = (j + k) % 4
            zsend[g, k, :, columns] = tsum[g, zi, :, columns].astype(BF)
            send(
                zsend.at[g, k, :, columns],
                zrecv.at[g, k, :, columns],
                SEM["gz"] + 4 * part + k,
                at_z(2 * zi + par),
            )

    def gram_end(part):
        g, first, width = GRAMS[part]
        columns = pl.ds(first, width)
        value = tsum[g, j, :, columns]
        for k in (1, 3, 2):
            arrived(zrecv.at[g, k, :, columns], SEM["gz"] + 4 * part + k)
            value = value + zrecv[g, k, :, columns].astype(F32)
        return value

    def field_rows(cc):
        return jnp.concatenate([f5[zi, xx, cc] for xx in range(X) for zi in range(4)], axis=0)

    s_arrive(0)
    s_begin(0)
    s_arrive(1)
    s_begin(1)
    w_take(1)
    w_take(2)
    s_arrive(2)
    s_begin(2)
    s_arrive(3)
    s_begin(3)
    w_relay(0)
    s_cross(0, 0)
    s_cross(0, 1)
    s_cross(1, 0)
    s_cross(1, 1)
    w_take(3)
    w_relay(1)
    s_arrive(4)
    s_begin(4)
    s_arrive(5)
    s_begin(5)
    w_relay(2)
    chosen = sp[q, 0, :, sub].astype(F32)
    for zi in range(1, 4):
        chosen = jnp.where(p == zi, sp[q, zi, :, sub].astype(F32), chosen)
    psp[slot] = chosen.astype(BF)
    panel_send(psp, SEM["ps"])
    s_cross(2, 0)
    s_cross(2, 1)
    s_cross(3, 0)
    s_cross(3, 1)
    w_take(4)
    w_relay(3)
    w_take(5)
    w_take(6)
    w_relay(4)
    s_cross(0, 2)
    s_cross(1, 2)
    s_cross(2, 2)
    s_cross(3, 2)
    panel_pass(psp, SEM["ps"])
    s_cross(4, 0)
    s_cross(4, 1)
    s_cross(5, 0)
    s_cross(5, 1)
    w_take(7)
    w_relay(5)
    for d in range(1, Z):
        arrived(eg.at[y, (z + d) % Z], SEM["ez"] + Z - d)
    for k in range(1, Y):
        send(eg.at[y], eg.at[y], SEM["ey"] + k, at_y(k))
    w_relay(6)
    panel_wait(psp, SEM["ps"], 0)
    panel_wait(psp, SEM["ps"], 1)
    gram_start(0, spin_rows, psp[...].reshape(PANEL_ROWS, 128))
    w_relay(7)
    s_cross(4, 2)
    s_cross(5, 2)
    gram_x(0)

    for u in range(6):
        s_end(u)
    total = None
    for i in range(Z):
        z1 = toward(NEAR[i])
        if i % 2 == 0:
            arrived(wg.at[z1 * Y + (y + 1) % Y], SEM["wy"] + 8 + i)
        else:
            arrived(wg.at[z1 * Y + (y + 3) % Y], SEM["wy"] + i)
        arrived(wg.at[z1 * Y + (y + 2) % Y], SEM["wy"] + 16 + i)
        term = jnp.dot(
            sp[z1].reshape(512, 512), wg[pl.ds(z1 * Y, Y)].reshape(512, 256), preferred_element_type=F32
        )
        total = term if total is None else total + term
    mine = bias[:, pl.ds(pl.multiple_of(j * 256, 256), 256)]
    fields = jnp.tanh(total + mine).astype(BF)
    f5[...] = fields.reshape(4, X, C, 16, 256)
    pf[slot] = f5[p].reshape(128, 256)
    panel_send(pf, SEM["pf"])

    fty[y] = fields.astype(F32).T.astype(BF)
    panel_pass(pf, SEM["pf"])
    for k in (1, 3, 2):
        t_send(k)
    send(fty.at[y], fty.at[y], SEM["fy"], at_y(1))
    send(fty.at[y], fty.at[y], SEM["fy"] + 1, at_y(3))
    panel_wait(pf, SEM["pf"], 0)
    gram_start(1, field_rows, pf[pl.ds(par * 4, 4)].reshape(512, 256))
    gram_x(1)
    for k in range(1, Y):
        arrived(eg.at[(y + 4 - k) % 4], SEM["ey"] + k)
    mean = jnp.sum(jnp.sum(eg[...].reshape(32, 128), axis=0, keepdims=True), axis=1, keepdims=True) / SAMPLES
    shifted = jnp.concatenate([eg[yy, 2 * p + zp] for zp in range(2) for yy in range(Y)], axis=1) - mean
    high = shifted.astype(BF).astype(F32)
    rest = shifted - high
    middle = rest.astype(BF).astype(F32)
    low = rest - middle
    row = lax.broadcasted_iota(jnp.int32, (16, PANEL_ROWS), 0)
    pieces = jnp.where(row == 0, high, jnp.where(row == 1, middle, jnp.where(row == 2, low, 0.0)))
    load_d.wait()
    solved = jnp.sum(
        lax.dot_general(pieces.astype(BF), dg[...], CONTRACT, preferred_element_type=F32), axis=0, keepdims=True
    )
    panel_wait(pf, SEM["pf"], 1)
    gram_start(2, field_rows, pf[pl.ds((1 - par) * 4, 4)].reshape(512, 256))
    gram_x(2)
    t_arrive(0)
    t_begin(0)
    t_begin(1)
    t_arrive(2)
    t_begin(4)
    t_begin(5)
    gram_z(0)
    gram_z(1)
    t_arrive(1)
    t_begin(2)
    t_begin(3)
    gram_z(2)
    for k in range(2):
        passed = fty.at[(y + (3, 1)[k]) % Y]
        arrived(passed, SEM["fy"] + k)
        part = fty.at[(y + (3, 1)[k]) % Y, pl.ds(128 * k, 128)]
        send(part, part, SEM["fy"] + 2 + k, at_y((1, 3)[k]))
    t_cross(0, 0)
    t_cross(0, 1)
    t_cross(1, 0)
    t_cross(1, 1)
    spin_total = gram_end(0)
    ftot[:, pl.ds(pl.multiple_of(par * 512, 512), 512)] = gram_end(1)
    ftot[:, pl.ds(pl.multiple_of((1 - par) * 512, 512), 512)] = gram_end(2)
    field_total = ftot[...]
    gram_column = (spin_total / SPIN_SITES * (field_total / HIDDEN_UNITS)).astype(BF)
    factor = lax.dot_general(gram_column, dg[...], CONTRACT, preferred_element_type=F32)
    factor_out[...] = factor.astype(BF)

    sample = lax.broadcasted_iota(jnp.int32, (16, PANEL_ROWS), 0)
    column = lax.broadcasted_iota(jnp.int32, (16, PANEL_ROWS), 1)
    picked = jnp.sum(
        jnp.where(column == slot * 128 + q * 16 + sample, solved, 0.0), axis=1, keepdims=True
    )
    carried = jnp.sum(factor * solved, axis=1, keepdims=True)
    narrow_row = lax.broadcasted_iota(jnp.int32, (16, 128), 0)
    narrow_col = lax.broadcasted_iota(jnp.int32, (16, 128), 1)
    here = narrow_col == q * 16 + narrow_row
    own = jnp.sum(jnp.where(here, energy_row, 0.0), axis=1, keepdims=True)
    in_panel = jnp.broadcast_to(p, (16, 1)) == j
    update = jnp.where(in_panel, picked, own - mean - carried)
    update_out[...] = jnp.sum(
        jnp.where(narrow_row == narrow_col, update, 0.0), axis=0, keepdims=True
    )
    u1[q] = jnp.sum(jnp.where(here, update, 0.0), axis=0, keepdims=True)
    for d in range(1, Q):
        send(u1.at[q], u1.at[q], SEM["uq"] + d, (wide, (q + d) % Q))
    t_cross(4, 0)
    t_cross(4, 1)
    t_cross(5, 0)
    t_cross(5, 1)
    t_cross(2, 0)
    t_cross(2, 1)
    t_cross(3, 0)
    t_cross(3, 1)
    for d in range(1, Q):
        arrived(u1.at[(q + Q - d) % Q], SEM["uq"] + d)
    u2[y, j] = jnp.sum(u1[...].reshape(Q, 128), axis=0, keepdims=True)
    plane = [(kz, ky) for kz in (0, 1, 3, 2) for ky in (0, 1, 3, 2)][1:]
    for kz, ky in plane:
        device = ((2 * ((j + kz) % 4) + par) * Y + (y + ky) % Y, q)
        send(u2.at[y, j], u2.at[y, j], SEM["up"] + 4 * kz + ky, device)
    for u in range(6):
        t_cross(u, 2)
    for u in range(6):
        t_end(u)
    for k in range(2):
        arrived(fty.at[(y + 2) % Y, pl.ds(128 * k, 128)], SEM["fy"] + 2 + k)
    for kz, ky in plane:
        arrived(u2.at[(y + 4 - ky) % Y, (j + 4 - kz) % 4], SEM["up"] + 4 * kz + ky)
    for yy in range(Y):
        coefficient = jnp.concatenate([u2[yy, zi] for zi in range(4)], axis=1)
        wt[yy] = (fty[yy].astype(F32) * coefficient).astype(BF)

    mine_y = pl.ds(pl.multiple_of(y * 128, 128), 128)

    def sites(o, k):
        if k == 0:
            return sp[toward(o), :, :, mine_y].reshape(512, 128)
        return s2[toward(o), (y + k) % Y].reshape(512, 128)

    def products(first, second):
        product = None
        for k in range(Y):
            both = jnp.concatenate([sites(first, k), sites(second, k)], axis=1)
            term = jnp.dot(wt[(y + k) % Y], both, preferred_element_type=F32)
            product = term if product is None else product + term
        return product[:, :128], product[:, 128:]

    def to_owner(o, value):
        seen = {1: 1, 2: -2, -1: -1, -3: -3, -2: 2}[o]
        zb[o + 3] = value.astype(BF)
        send(zb.at[o + 3], r3.at[z], SEM["r3"] + 3 + seen, at_z(toward(o)))

    for n in range(2):
        away, near = products(4 - n, n - 3)
        zb[7 - n] = away.astype(BF)
        send(zb.at[7 - n], rel.at[n], SEM["rel"] + n, at_z(partner))
        nearsum[n] = near

    def relay_sum(n):
        arrived(rel.at[n], SEM["rel"] + n)
        to_owner(n - 3, nearsum[n] + rel[n].astype(F32))

    ahead, behind = products(2, -1)
    to_owner(2, ahead)
    to_owner(-1, behind)
    ahead, own_term = products(1, 0)
    r3[z] = own_term.astype(BF)
    relay_sum(0)
    relay_sum(1)
    to_owner(1, ahead)
    for o in (-3, 2, -2, -1, 1):
        arrived(r3.at[toward(o)], SEM["r3"] + 3 + o)
    for copy in sends:
        copy.wait_send()


def finish(terms, factor, update, grad_out, factor_out, update_out):
    factor_out[...] = factor[...]
    update_out[...] = update[0, :16]
    for jj in range(4):
        block = terms[2 * jj].astype(F32) + terms[2 * jj + 1].astype(F32)
        grad_out[:, jj * 256 : (jj + 1) * 256] = block.T / math.sqrt(SAMPLES)


def local(spins, weights, field_bias, energies, panel_index, diag_inverse):
    vmem = pl.BlockSpec(memory_space=pltpu.VMEM)
    anywhere = pl.BlockSpec(memory_space=pl.ANY)
    smem = pl.BlockSpec(memory_space=pltpu.SMEM)
    terms, factor, update = pl.pallas_call(
        kernel,
        out_shape=(
            jax.ShapeDtypeStruct((Z, 256, 128), BF),
            jax.ShapeDtypeStruct((16, PANEL_ROWS), BF),
            jax.ShapeDtypeStruct((1, 128), F32),
        ),
        in_specs=[anywhere, anywhere, vmem, vmem, smem, anywhere],
        out_specs=(vmem, vmem, vmem),
        scratch_shapes=[
            pltpu.VMEM((Q, 128, 512), jnp.int32),
            pltpu.VMEM((Q, 4, 128, 512), BF),
            pltpu.VMEM((32, 128, 256), BF),
            pltpu.VMEM((PANEL_ROWS, PANEL_ROWS), BF),
            pltpu.VMEM((4, X, C, 16, 256), BF),
            pltpu.VMEM((Y, Z, 1, 128), F32),
            pltpu.VMEM((8, 128, 128), BF),
            pltpu.VMEM((8, 128, 256), BF),
            pltpu.VMEM((16, PANEL_ROWS), F32),
            pltpu.VMEM((2, 256, PANEL_ROWS), BF),
            pltpu.VMEM((2, 256, PANEL_ROWS), F32),
            pltpu.VMEM((2, 256, PANEL_ROWS), BF),
            pltpu.VMEM((2, 4, 64, PANEL_ROWS), BF),
            pltpu.VMEM((2, 4, 64, PANEL_ROWS), BF),
            pltpu.VMEM((2, 4, 16, PANEL_ROWS), F32),
            pltpu.VMEM((2, 4, 16, PANEL_ROWS), BF),
            pltpu.VMEM((2, 4, 16, PANEL_ROWS), BF),
            pltpu.VMEM((Q, 1, 128), F32),
            pltpu.VMEM((Y, 4, 1, 128), F32),
            pltpu.VMEM((Y, 256, 512), BF),
            pltpu.VMEM((Q, Y, 4, 128, 128), BF),
            pltpu.VMEM((Y, 256, 512), BF),
            pltpu.VMEM((Z, 256, 128), BF),
            pltpu.VMEM((2, 256, 128), BF),
            pltpu.VMEM((2, 256, 128), F32),
            pltpu.SemaphoreType.DMA((NSEM,)),
            pltpu.SemaphoreType.DMA((NSEM,)),
            pltpu.SemaphoreType.DMA((10,)),
        ],
        compiler_params=pltpu.CompilerParams(
            collective_id=0, has_side_effects=True, vmem_limit_bytes=56 * 1024 * 1024
        ),
    )(
        spins,
        weights,
        field_bias.reshape(1, -1),
        energies,
        panel_index,
        diag_inverse,
    )
    return pl.pallas_call(
        finish,
        out_shape=(
            jax.ShapeDtypeStruct((128, 1024), F32),
            jax.ShapeDtypeStruct((16, PANEL_ROWS), BF),
            jax.ShapeDtypeStruct((16,), F32),
        ),
        in_specs=[vmem, vmem, vmem],
        out_specs=(vmem, vmem, vmem),
    )(terms, factor, update)


def solution(mesh):
    in_specs = (P("wide", None), P("wide", "narrow"), P("narrow"), P("wide"), P(), P())
    out_specs = (P("wide", "narrow"), P(("wide", "narrow"), None), P(("wide", "narrow")))
    return jax.shard_map(local, mesh=mesh, in_specs=in_specs, out_specs=out_specs, check_vma=False)
```

```python
import functools
import math

import jax
import jax.numpy as jnp
from jax import lax
from jax.experimental import pallas as pl
from jax.experimental.pallas import tpu as pltpu
from jax.sharding import PartitionSpec as P

SPIN_SITES = 4096
HIDDEN_UNITS = 8192
PANEL_ROWS = 1024
SAMPLES = 4096
Z, Y, X, C = 8, 4, 4, 2
Q = X * C
NEAR = (0, 1, -1, -2, 2, -3, 3, 4)
SAME = (2, 6, 4)
GRAMS = ((0, 0, 1024), (1, 0, 512), (1, 512, 512))
UNITS = ((0, 0), (1, 1), (0, 1), (1, 0), (2, 0), (2, 1))
MESH = pl.DeviceIdType.MESH
BF = jnp.bfloat16
F32 = jnp.float32
CONTRACT = (((1,), (1,)), ((), ()))


class Sems:
    def __init__(self):
        self.n = 0

    def take(self, n):
        self.n += n
        return self.n - n


def layout():
    s = Sems()
    names = dict(
        wz=8, wy=24, sz=6, sx=18, sc=24, ty=4, tx=18, tc=24, ez=8, ey=4, ps=7, pf=7, fy=4,
        gc=3, gx=12, gz=12, uq=8, up=16, r3=8, rel=2,
    )
    return {k: s.take(n) for k, n in names.items()}, s.n


SEM, NSEM = layout()


def kernel(
    spins, weights, bias, energy, panel, diag,
    r3, factor_out, update_out,
    s32, sp, wg, dg, f5, eg, psp, pf,
    ftot, gsend, gkeep, grecv, xsend, xrecv, tsum, zsend, zrecv,
    u1, u2, wt, s2, fty, zb, rel, nearsum,
    ssem, rsem, lsem,
):
    wide = lax.axis_index("wide")
    q = lax.axis_index("narrow")
    z, y = wide // Y, wide % Y
    x, c = q // C, q % C
    par, j = z % 2, z // 2
    sib = x * C + (1 - c)
    sign = 1 - 2 * par
    partner = z + sign
    sends = []

    def at_z(zz):
        return (zz * Y + y, q)

    def at_y(k):
        return (z * Y + (y + k) % Y, q)

    def at_x(k):
        return (wide, ((x + k) % X) * C + c)

    def send(src, dst, index, device):
        copy = pltpu.make_async_remote_copy(
            src_ref=src, dst_ref=dst, send_sem=ssem.at[index], recv_sem=rsem.at[index],
            device_id=device, device_id_type=MESH,
        )
        copy.start()
        sends.append(copy)

    def arrived(dst, index):
        pltpu.make_async_remote_copy(
            src_ref=dst, dst_ref=dst, send_sem=ssem.at[index], recv_sem=rsem.at[index],
            device_id=(wide, sib), device_id_type=MESH,
        ).wait_recv()

    def load_spins(k):
        return pltpu.make_async_copy(spins.at[:, pl.ds(pl.multiple_of(k * 512, 512), 512)], s32.at[k], lsem.at[k])

    for d in range(Q):
        load_spins((q + d) % Q).start()
    my_w = weights.at[:, pl.ds(pl.multiple_of(j * 256, 256), 256)]
    load_w = pltpu.make_async_copy(my_w, wg.at[wide], lsem.at[8])
    load_w.start()
    load_d = pltpu.make_async_copy(diag, dg, lsem.at[9])
    load_d.start()

    barrier = pltpu.get_barrier_semaphore()
    for d in range(1, Z):
        pl.semaphore_signal(barrier, inc=1, device_id=at_z((z + d) % Z), device_id_type=MESH)
    for k in range(1, Y):
        pl.semaphore_signal(barrier, inc=1, device_id=at_y(k), device_id_type=MESH)
    for d in range(1, Q):
        pl.semaphore_signal(barrier, inc=1, device_id=(wide, (q + d) % Q), device_id_type=MESH)

    def convert(k):
        load_spins(k).wait()
        sp[k, j] = s32[k].astype(F32).astype(BF)

    convert(q)
    energy_row = energy[...].astype(F32).reshape(1, 128)
    eg[y, z] = energy_row
    load_w.wait()
    pl.semaphore_wait(barrier, Z + Y + Q - 3)

    def w_y(i, z1):
        chunk = wg.at[z1 * Y + y]
        send(chunk, chunk, SEM["wy"] + i, at_y(1))
        send(chunk, chunk, SEM["wy"] + 8 + i, at_y(-1 + Y))

    def toward(o):
        return (z + sign * o + Z) % Z

    def w_z(o):
        zd = toward(o)
        src = weights.at[:, pl.ds(pl.multiple_of((zd // 2) * 256, 256), 256)]
        seen = {1: 1, -1: -1, 2: -2, -3: -3}[o]
        send(src, wg.at[wide], SEM["wz"] + 3 + seen, at_z(zd))

    def s_z(u):
        t, h = UNITS[u]
        mine = sp.at[q, j, pl.ds(64 * h, 64)]
        send(mine, mine, SEM["sz"] + u, at_z((z + (6, 2)[t]) % Z))

    w_y(0, z)
    s_z(0)
    s_z(1)
    w_z(1)
    w_z(-1)
    s_z(2)
    s_z(3)
    w_z(2)
    w_z(-3)
    for d in range(1, Z):
        send(eg.at[y, z], eg.at[y, z], SEM["ez"] + d, at_z((z + d) % Z))
    for d in range(1, Q):
        convert((q + d) % Q)
    for o in (3, 4):
        r3[toward(o)] = jnp.zeros((256, 128), BF)

    def w_take(i):
        o = NEAR[i]
        z1 = toward(o)
        chunk = wg.at[z1 * Y + y]
        arrived(chunk, SEM["wz"] + 3 + o)
        if o < 0:
            send(chunk, chunk, SEM["wz"] + 4 - o, at_z(partner))
        w_y(i, z1)

    def w_relay(i):
        z1 = toward(NEAR[i])
        if i % 2 == 0:
            chunk = wg.at[z1 * Y + (y + 3) % Y]
            arrived(chunk, SEM["wy"] + i)
            send(chunk, chunk, SEM["wy"] + 16 + i, at_y(1))
        else:
            chunk = wg.at[z1 * Y + (y + 1) % Y]
            arrived(chunk, SEM["wy"] + 8 + i)
            send(chunk, chunk, SEM["wy"] + 16 + i, at_y(3))

    def zi_of(t):
        return ((z + SAME[t]) % Z) // 2

    def s_piece(source, u):
        t, h = UNITS[u]
        return sp.at[source, zi_of(t), pl.ds(64 * h, 64)]

    def s_arrive(u):
        got = s_piece(q, u)
        arrived(got, SEM["sz"] + u)
        if u < 2:
            send(got, got, SEM["sz"] + 4 + u, at_z((z + (6, 2)[u]) % Z))

    def spread(piece, bx, bc):
        def begin(u):
            mine = piece(q, u)
            send(mine, mine, bx + u, at_x(1))
            send(mine, mine, bx + 6 + u, at_x(3))
            send(mine, mine, bc + u, (wide, sib))

        def cross(u, k):
            source = ((x + (3, 1, 2)[k]) % X) * C + c
            got = piece(source, u)
            arrived(got, bx + 6 * k + u)
            if k == u % 2:
                send(got, got, bx + 12 + u, at_x((1, 3)[k]))
            send(got, got, bc + 6 * (k + 1) + u, (wide, sib))

        def end(u):
            for k in range(4):
                source = ((x + (0, 3, 1, 2)[k]) % X) * C + (1 - c)
                arrived(piece(source, u), bc + 6 * k + u)

        return begin, cross, end

    s_begin, s_cross, s_end = spread(s_piece, SEM["sx"], SEM["sc"])
    t_begin, t_cross, t_end = spread(
        lambda source, u: s2.at[source, (y + u // 2 + 1) % Y, pl.ds(2 * (u % 2), 2)], SEM["tx"], SEM["tc"]
    )

    def t_send(k):
        columns = pl.ds(pl.multiple_of(((y + k) % Y) * 128, 128), 128)
        send(sp.at[q, :, :, columns], s2.at[q, y], SEM["ty"] + k, at_y(k))

    def t_arrive(t):
        arrived(s2.at[q, (y + t + 1) % Y], SEM["ty"] + Y - 1 - t)

    p = panel[0]
    slot = par * 4 + y
    other = (1 - par) * 4 + y

    def panel_send(buf, base):
        send(buf.at[slot], buf.at[slot], base, at_z(partner))
        for k in (1, 3, 2):
            send(buf.at[slot], buf.at[slot], base + k, at_y(k))

    def panel_pass(buf, base):
        arrived(buf.at[other], base)
        for k in (1, 3, 2):
            send(buf.at[other], buf.at[other], base + 3 + k, at_y(k))

    def panel_wait(buf, base, half):
        for k in (1, 3, 2):
            group = (1 - par) if half else par
            arrived(buf.at[group * 4 + (y + 4 - k) % 4], base + 3 * half + k)

    sub = pl.ds(pl.multiple_of(j * 128, 128), 128)

    def gram_start(part, rows_of, rhs):
        g, first, width = GRAMS[part]
        columns = pl.ds(first, width)
        theirs = lax.dot_general(rows_of(1 - c), rhs, CONTRACT, preferred_element_type=F32)
        gsend[g, :, columns] = theirs.astype(BF)
        send(gsend.at[g, :, columns], grecv.at[g, :, columns], SEM["gc"] + part, (wide, sib))
        gkeep[g, :, columns] = lax.dot_general(rows_of(c), rhs, CONTRACT, preferred_element_type=F32)

    def spin_rows(cc):
        return jnp.concatenate(
            [
                sp[q, zi, pl.ds(pl.multiple_of((2 * xx + cc) * 16, 16), 16), sub]
                for xx in range(X)
                for zi in range(4)
            ],
            axis=0,
        )

    def gram_x(part):
        g, first, width = GRAMS[part]
        columns = pl.ds(first, width)
        arrived(grecv.at[g, :, columns], SEM["gc"] + part)
        for k in (2, 1, 3):
            rows = pl.ds(pl.multiple_of(((x + k) % X) * 64, 64), 64)
            value = gkeep[g, rows, columns] + grecv[g, rows, columns].astype(F32)
            xsend[g, k, :, columns] = value.astype(BF)
            send(xsend.at[g, k, :, columns], xrecv.at[g, k, :, columns], SEM["gx"] + 4 * part + k, at_x(k))

    def gram_z(part):
        g, first, width = GRAMS[part]
        columns = pl.ds(first, width)
        rows = pl.ds(pl.multiple_of(x * 64, 64), 64)
        value = gkeep[g, rows, columns] + grecv[g, rows, columns].astype(F32)
        for k in (1, 3, 2):
            arrived(xrecv.at[g, k, :, columns], SEM["gx"] + 4 * part + k)
            value = value + xrecv[g, k, :, columns].astype(F32)
        tsum[g, :, :, columns] = value.reshape(4, 16, width)
        for k in (2, 1, 3):
            zi = (j + k) % 4
            zsend[g, k, :, columns] = tsum[g, zi, :, columns].astype(BF)
            send(
                zsend.at[g, k, :, columns],
                zrecv.at[g, k, :, columns],
                SEM["gz"] + 4 * part + k,
                at_z(2 * zi + par),
            )

    def gram_end(part):
        g, first, width = GRAMS[part]
        columns = pl.ds(first, width)
        value = tsum[g, j, :, columns]
        for k in (1, 3, 2):
            arrived(zrecv.at[g, k, :, columns], SEM["gz"] + 4 * part + k)
            value = value + zrecv[g, k, :, columns].astype(F32)
        return value

    def field_rows(cc):
        return jnp.concatenate([f5[zi, xx, cc] for xx in range(X) for zi in range(4)], axis=0)

    s_arrive(0)
    s_begin(0)
    s_arrive(1)
    s_begin(1)
    w_take(1)
    w_take(2)
    s_arrive(2)
    s_begin(2)
    s_arrive(3)
    s_begin(3)
    w_relay(0)
    s_cross(0, 0)
    s_cross(0, 1)
    s_cross(1, 0)
    s_cross(1, 1)
    w_take(3)
    w_relay(1)
    s_arrive(4)
    s_begin(4)
    s_arrive(5)
    s_begin(5)
    w_relay(2)
    chosen = sp[q, 0, :, sub].astype(F32)
    for zi in range(1, 4):
        chosen = jnp.where(p == zi, sp[q, zi, :, sub].astype(F32), chosen)
    psp[slot] = chosen.astype(BF)
    panel_send(psp, SEM["ps"])
    s_cross(2, 0)
    s_cross(2, 1)
    s_cross(3, 0)
    s_cross(3, 1)
    w_take(4)
    w_relay(3)
    w_take(5)
    w_take(6)
    w_relay(4)
    s_cross(0, 2)
    s_cross(1, 2)
    s_cross(2, 2)
    s_cross(3, 2)
    panel_pass(psp, SEM["ps"])
    s_cross(4, 0)
    s_cross(4, 1)
    s_cross(5, 0)
    s_cross(5, 1)
    w_take(7)
    w_relay(5)
    for d in range(1, Z):
        arrived(eg.at[y, (z + d) % Z], SEM["ez"] + Z - d)
    for k in range(1, Y):
        send(eg.at[y], eg.at[y], SEM["ey"] + k, at_y(k))
    w_relay(6)
    panel_wait(psp, SEM["ps"], 0)
    panel_wait(psp, SEM["ps"], 1)
    gram_start(0, spin_rows, psp[...].reshape(PANEL_ROWS, 128))
    w_relay(7)
    s_cross(4, 2)
    s_cross(5, 2)
    gram_x(0)

    for u in range(6):
        s_end(u)
    total = None
    for i in range(Z):
        z1 = toward(NEAR[i])
        if i % 2 == 0:
            arrived(wg.at[z1 * Y + (y + 1) % Y], SEM["wy"] + 8 + i)
        else:
            arrived(wg.at[z1 * Y + (y + 3) % Y], SEM["wy"] + i)
        arrived(wg.at[z1 * Y + (y + 2) % Y], SEM["wy"] + 16 + i)
        term = jnp.dot(
            sp[z1].reshape(512, 512), wg[pl.ds(z1 * Y, Y)].reshape(512, 256), preferred_element_type=F32
        )
        total = term if total is None else total + term
    mine = bias[:, pl.ds(pl.multiple_of(j * 256, 256), 256)]
    fields = jnp.tanh(total + mine).astype(BF)
    f5[...] = fields.reshape(4, X, C, 16, 256)
    pf[slot] = f5[p].reshape(128, 256)
    panel_send(pf, SEM["pf"])

    fty[y] = fields.astype(F32).T.astype(BF)
    panel_pass(pf, SEM["pf"])
    for k in (1, 3, 2):
        t_send(k)
    send(fty.at[y], fty.at[y], SEM["fy"], at_y(1))
    send(fty.at[y], fty.at[y], SEM["fy"] + 1, at_y(3))
    panel_wait(pf, SEM["pf"], 0)
    gram_start(1, field_rows, pf[pl.ds(par * 4, 4)].reshape(512, 256))
    gram_x(1)
    for k in range(1, Y):
        arrived(eg.at[(y + 4 - k) % 4], SEM["ey"] + k)
    mean = jnp.sum(jnp.sum(eg[...].reshape(32, 128), axis=0, keepdims=True), axis=1, keepdims=True) / SAMPLES
    shifted = jnp.concatenate([eg[yy, 2 * p + zp] for zp in range(2) for yy in range(Y)], axis=1) - mean
    high = shifted.astype(BF).astype(F32)
    rest = shifted - high
    middle = rest.astype(BF).astype(F32)
    low = rest - middle
    row = lax.broadcasted_iota(jnp.int32, (16, PANEL_ROWS), 0)
    pieces = jnp.where(row == 0, high, jnp.where(row == 1, middle, jnp.where(row == 2, low, 0.0)))
    load_d.wait()
    solved = jnp.sum(
        lax.dot_general(pieces.astype(BF), dg[...], CONTRACT, preferred_element_type=F32), axis=0, keepdims=True
    )
    panel_wait(pf, SEM["pf"], 1)
    gram_start(2, field_rows, pf[pl.ds((1 - par) * 4, 4)].reshape(512, 256))
    gram_x(2)
    t_arrive(0)
    t_begin(0)
    t_begin(1)
    t_arrive(2)
    t_begin(4)
    t_begin(5)
    gram_z(0)
    gram_z(1)
    t_arrive(1)
    t_begin(2)
    t_begin(3)
    gram_z(2)
    for k in range(2):
        passed = fty.at[(y + (3, 1)[k]) % Y]
        arrived(passed, SEM["fy"] + k)
        part = fty.at[(y + (3, 1)[k]) % Y, pl.ds(128 * k, 128)]
        send(part, part, SEM["fy"] + 2 + k, at_y((1, 3)[k]))
    t_cross(0, 0)
    t_cross(0, 1)
    t_cross(1, 0)
    t_cross(1, 1)
    spin_total = gram_end(0)
    ftot[:, pl.ds(pl.multiple_of(par * 512, 512), 512)] = gram_end(1)
    ftot[:, pl.ds(pl.multiple_of((1 - par) * 512, 512), 512)] = gram_end(2)
    field_total = ftot[...]
    gram_column = (spin_total / SPIN_SITES * (field_total / HIDDEN_UNITS)).astype(BF)
    factor = lax.dot_general(gram_column, dg[...], CONTRACT, preferred_element_type=F32)
    factor_out[...] = factor.astype(BF)

    sample = lax.broadcasted_iota(jnp.int32, (16, PANEL_ROWS), 0)
    column = lax.broadcasted_iota(jnp.int32, (16, PANEL_ROWS), 1)
    picked = jnp.sum(
        jnp.where(column == slot * 128 + q * 16 + sample, solved, 0.0), axis=1, keepdims=True
    )
    carried = jnp.sum(factor * solved, axis=1, keepdims=True)
    narrow_row = lax.broadcasted_iota(jnp.int32, (16, 128), 0)
    narrow_col = lax.broadcasted_iota(jnp.int32, (16, 128), 1)
    here = narrow_col == q * 16 + narrow_row
    own = jnp.sum(jnp.where(here, energy_row, 0.0), axis=1, keepdims=True)
    in_panel = jnp.broadcast_to(p, (16, 1)) == j
    update = jnp.where(in_panel, picked, own - mean - carried)
    update_out[...] = jnp.sum(
        jnp.where(narrow_row == narrow_col, update, 0.0), axis=0, keepdims=True
    )
    u1[q] = jnp.sum(jnp.where(here, update, 0.0), axis=0, keepdims=True)
    for d in range(1, Q):
        send(u1.at[q], u1.at[q], SEM["uq"] + d, (wide, (q + d) % Q))
    t_cross(4, 0)
    t_cross(4, 1)
    t_cross(5, 0)
    t_cross(5, 1)
    t_cross(2, 0)
    t_cross(2, 1)
    t_cross(3, 0)
    t_cross(3, 1)
    for d in range(1, Q):
        arrived(u1.at[(q + Q - d) % Q], SEM["uq"] + d)
    u2[y, j] = jnp.sum(u1[...].reshape(Q, 128), axis=0, keepdims=True)
    plane = [(kz, ky) for kz in (0, 1, 3, 2) for ky in (0, 1, 3, 2)][1:]
    for kz, ky in plane:
        device = ((2 * ((j + kz) % 4) + par) * Y + (y + ky) % Y, q)
        send(u2.at[y, j], u2.at[y, j], SEM["up"] + 4 * kz + ky, device)
    for u in range(6):
        t_cross(u, 2)
    for u in range(6):
        t_end(u)
    for k in range(2):
        arrived(fty.at[(y + 2) % Y, pl.ds(128 * k, 128)], SEM["fy"] + 2 + k)
    for kz, ky in plane:
        arrived(u2.at[(y + 4 - ky) % Y, (j + 4 - kz) % 4], SEM["up"] + 4 * kz + ky)
    for yy in range(Y):
        coefficient = jnp.concatenate([u2[yy, zi] for zi in range(4)], axis=1)
        wt[yy] = (fty[yy].astype(F32) * coefficient).astype(BF)

    mine_y = pl.ds(pl.multiple_of(y * 128, 128), 128)

    def sites(o, k):
        if k == 0:
            return sp[toward(o), :, :, mine_y].reshape(512, 128)
        return s2[toward(o), (y + k) % Y].reshape(512, 128)

    def products(first, second):
        product = None
        for k in range(Y):
            both = jnp.concatenate([sites(first, k), sites(second, k)], axis=1)
            term = jnp.dot(wt[(y + k) % Y], both, preferred_element_type=F32)
            product = term if product is None else product + term
        return product[:, :128], product[:, 128:]

    def to_owner(o, value):
        seen = {1: 1, 2: -2, -1: -1, -3: -3, -2: 2}[o]
        zb[o + 3] = value.astype(BF)
        send(zb.at[o + 3], r3.at[z], SEM["r3"] + 3 + seen, at_z(toward(o)))

    for n in range(2):
        away, near = products(4 - n, n - 3)
        zb[7 - n] = away.astype(BF)
        send(zb.at[7 - n], rel.at[n], SEM["rel"] + n, at_z(partner))
        nearsum[n] = near

    def relay_sum(n):
        arrived(rel.at[n], SEM["rel"] + n)
        to_owner(n - 3, nearsum[n] + rel[n].astype(F32))

    ahead, behind = products(2, -1)
    to_owner(2, ahead)
    to_owner(-1, behind)
    ahead, own_term = products(1, 0)
    r3[z] = own_term.astype(BF)
    relay_sum(0)
    relay_sum(1)
    to_owner(1, ahead)
    for o in (-3, 2, -2, -1, 1):
        arrived(r3.at[toward(o)], SEM["r3"] + 3 + o)
    for copy in sends:
        copy.wait_send()


def finish(terms, factor, update, grad_out, factor_out, update_out):
    factor_out[...] = factor[...]
    update_out[...] = update[0, :16]
    block = terms[0].astype(F32) + terms[1].astype(F32)
    grad_out[...] = block.T / math.sqrt(SAMPLES)


def local(spins, weights, field_bias, energies, panel_index, diag_inverse):
    vmem = pl.BlockSpec(memory_space=pltpu.VMEM)
    anywhere = pl.BlockSpec(memory_space=pl.ANY)
    smem = pl.BlockSpec(memory_space=pltpu.SMEM)
    terms, factor, update = pl.pallas_call(
        kernel,
        out_shape=(
            jax.ShapeDtypeStruct((Z, 256, 128), BF),
            jax.ShapeDtypeStruct((16, PANEL_ROWS), BF),
            jax.ShapeDtypeStruct((1, 128), F32),
        ),
        in_specs=[anywhere, anywhere, vmem, vmem, smem, anywhere],
        out_specs=(vmem, vmem, vmem),
        scratch_shapes=[
            pltpu.VMEM((Q, 128, 512), jnp.int32),
            pltpu.VMEM((Q, 4, 128, 512), BF),
            pltpu.VMEM((32, 128, 256), BF),
            pltpu.VMEM((PANEL_ROWS, PANEL_ROWS), BF),
            pltpu.VMEM((4, X, C, 16, 256), BF),
            pltpu.VMEM((Y, Z, 1, 128), F32),
            pltpu.VMEM((8, 128, 128), BF),
            pltpu.VMEM((8, 128, 256), BF),
            pltpu.VMEM((16, PANEL_ROWS), F32),
            pltpu.VMEM((2, 256, PANEL_ROWS), BF),
            pltpu.VMEM((2, 256, PANEL_ROWS), F32),
            pltpu.VMEM((2, 256, PANEL_ROWS), BF),
            pltpu.VMEM((2, 4, 64, PANEL_ROWS), BF),
            pltpu.VMEM((2, 4, 64, PANEL_ROWS), BF),
            pltpu.VMEM((2, 4, 16, PANEL_ROWS), F32),
            pltpu.VMEM((2, 4, 16, PANEL_ROWS), BF),
            pltpu.VMEM((2, 4, 16, PANEL_ROWS), BF),
            pltpu.VMEM((Q, 1, 128), F32),
            pltpu.VMEM((Y, 4, 1, 128), F32),
            pltpu.VMEM((Y, 256, 512), BF),
            pltpu.VMEM((Q, Y, 4, 128, 128), BF),
            pltpu.VMEM((Y, 256, 512), BF),
            pltpu.VMEM((Z, 256, 128), BF),
            pltpu.VMEM((2, 256, 128), BF),
            pltpu.VMEM((2, 256, 128), F32),
            pltpu.SemaphoreType.DMA((NSEM,)),
            pltpu.SemaphoreType.DMA((NSEM,)),
            pltpu.SemaphoreType.DMA((10,)),
        ],
        compiler_params=pltpu.CompilerParams(
            collective_id=0, has_side_effects=True, vmem_limit_bytes=56 * 1024 * 1024
        ),
    )(
        spins,
        weights,
        field_bias.reshape(1, -1),
        energies,
        panel_index,
        diag_inverse,
    )
    return pl.pallas_call(
        finish,
        out_shape=(
            jax.ShapeDtypeStruct((128, 1024), F32),
            jax.ShapeDtypeStruct((16, PANEL_ROWS), BF),
            jax.ShapeDtypeStruct((16,), F32),
        ),
        grid=(4,),
        in_specs=[pl.BlockSpec((2, 256, 128), lambda i: (i, 0, 0)), vmem, vmem],
        out_specs=(pl.BlockSpec((128, 256), lambda i: (0, i)), vmem, vmem),
    )(terms, factor, update)


def solution(mesh):
    in_specs = (P("wide", None), P("wide", "narrow"), P("narrow"), P("wide"), P(), P())
    out_specs = (P("wide", "narrow"), P(("wide", "narrow"), None), P(("wide", "narrow")))
    return jax.shard_map(local, mesh=mesh, in_specs=in_specs, out_specs=out_specs, check_vma=False)
```
